512 devices in a mesh: seq: 64 (over z, x, y_hi), tp: 8 (over y_lo, core).
Axes of the slice: x: 4, y: 8 (y_hi: 2, y_lo: 4; y = y_hi * 4 + y_lo), z: 8, core: 2. Of those that a mesh axis runs over, the one named last changes fastest.
Arguments:
- branches: bfloat16 [3, 16384, 4096], P(None, 'seq', 'tp'), may hold values from -6 to 6
- short_taps: float32 [3, 3, 4096], P(None, None, 'tp'), may hold values from -3 to 3
- skip_gain: float32 [4096], P('tp'), may hold values from -4 to 4
- long_filter: float32 [16384, 4096], P('seq', 'tp'), may hold values from -4 to 4
- out_weight: bfloat16 [4096, 4096], P('seq', 'tp'), may hold values from -0.09375 to 0.09375
Outputs:
- block_out: bfloat16 [16384, 4096], P('seq', 'tp')
The draws below stay inside these ranges and needn't reach their ends.
All inputs are finite; a program needn't handle non-finite values.
Results may differ from the reference program's by a relative error of at most 0.0049.
Values may be sent and summed in bfloat16 or wider, within the bound.
A program may use at most 64 MiB of HBM per device.

```python
import math
import jax
import jax.numpy as jnp
from jax import lax

D = 4096
CH = 4096
SEQ = 16384


def draw_long_filter(key, part):
    key = jax.random.fold_in(key, 7)
    rate_key, value_key = jax.random.split(key)
    rates = jnp.exp(jax.random.uniform(rate_key, (CH,), jnp.float32, math.log(0.5), math.log(4.0)))
    position = jnp.arange(SEQ, dtype=jnp.float32)[:, None] / float(SEQ)
    envelope = jnp.exp(-rates[None, :] * position)
    values = jnp.clip(jax.random.normal(value_key, (SEQ, CH), jnp.float32), -4.0, 4.0)
    return values * envelope


def block_scale(key, extent, pieces, low, largest):
    factor_of, own = 1.0, jax.random.fold_in(key, 6)
    for dim, parts in pieces:
        heights = jnp.exp(jax.random.uniform(jax.random.fold_in(own, dim), (parts,), jnp.float32, low / len(pieces), largest / len(pieces)))
        factor_of = factor_of * jnp.repeat(heights, extent[dim] // parts).reshape([-1 if axis == dim else 1 for axis in range(len(extent))])
    return factor_of


def noise(own_key, dims, deviation, bound, cuts=(), held_as=jnp.bfloat16):
    factor_of = block_scale(own_key, dims, cuts, -0.22, 0.18) if cuts else 1.0
    entries = jax.random.normal(own_key, dims, jnp.float32) * deviation * factor_of
    return jnp.minimum(jnp.maximum(entries, -bound), bound).astype(held_as)


def setup_inputs(seed: int = 0) -> dict:
    streams_of = jax.random.split(jax.random.key(seed), 6)
    branches = noise(streams_of[0], (3, SEQ, CH), 1.0, 6.0, ((1, 64), (2, 8)))
    short_taps = noise(streams_of[1], (3, 3, CH), 0.6, 3.0, ((2, 8),), jnp.float32)
    skip_gain = noise(streams_of[2], (CH,), 1.0, 4.0, ((0, 8),), jnp.float32)
    long_filter = draw_long_filter(jax.random.fold_in(streams_of[5], 71), 0)
    out_weight = noise(streams_of[4], (CH, D), CH ** -0.5, 0.09375, ((0, 64), (1, 8)))
    return dict(branches=branches, short_taps=short_taps, skip_gain=skip_gain, long_filter=long_filter, out_weight=out_weight)


def reference(branches, short_taps, skip_gain, long_filter, out_weight):
    length = branches.shape[1]
    projected = branches.astype(jnp.float32)
    padded = jnp.pad(projected, ((0, 0), (2, 0), (0, 0)))
    mixed = jnp.zeros((3, length, CH), jnp.float32)
    for tap_index in range(3):
        mixed = mixed + short_taps[tap_index][:, None, :] * padded[:, 2 - tap_index:2 - tap_index + length, :]
    signal = mixed[1] * mixed[2]
    kernel = long_filter.astype(jnp.float32)
    block = math.gcd(CH, 256)
    groups = CH // block
    signal_blocks = jnp.transpose(signal.reshape(length, groups, block), (1, 0, 2))
    kernel_blocks = jnp.transpose(kernel.reshape(length, groups, block), (1, 0, 2))

    def convolve(pair):
        spectrum = jnp.fft.rfft(pair[0], n=2 * length, axis=0) * jnp.fft.rfft(pair[1], n=2 * length, axis=0)
        return jnp.fft.irfft(spectrum, n=2 * length, axis=0)[:length]
    convolved = lax.map(convolve, (signal_blocks, kernel_blocks))
    convolved = jnp.transpose(convolved, (1, 0, 2)).reshape(length, CH) / math.sqrt(float(length))
    gated = (mixed[0] * (convolved + skip_gain[None] * signal)).astype(jnp.bfloat16)
    return jnp.dot(gated, out_weight, preferred_element_type=jnp.float32).astype(jnp.bfloat16)
```

```python
import functools
import math

import jax
import jax.numpy as jnp
from jax import lax
from jax.experimental import pallas as pl
from jax.experimental.pallas import tpu as pltpu
from jax.sharding import PartitionSpec as P

MESH = pl.DeviceIdType.MESH
LANES = 128
GROUP = 8
SHIFTS = 16


def ring_sizes(seq_size):
    return (seq_size // 8, 4, 2) if seq_size >= 32 else (seq_size // 4, 2, 2)


def place(seq_size):
    nz, nx, ny = ring_sizes(seq_size)
    me = lax.axis_index("seq")
    return me // (nx * ny), (me // ny) % nx, me % ny


def remote(src, dst, send_sem, recv_sem, device_id):
    return pltpu.make_async_remote_copy(
        src_ref=src,
        dst_ref=dst,
        send_sem=send_sem,
        recv_sem=recv_sem,
        device_id=device_id,
        device_id_type=MESH,
    )


def scatter_start(send, land, send_sem, recv_sem):
    count = send.shape[0]
    me = lax.axis_index("seq")

    def step(t, carry):
        peer = lax.rem(me + t, count)
        remote(send.at[peer], land.at[me], send_sem, recv_sem, {"seq": peer}).start()
        return carry

    lax.fori_loop(1, count, step, 0)
    land[me] = send[me]


def scatter_wait(send, land, send_sem, recv_sem):
    others = pl.ds(0, send.shape[0] - 1)
    copy = remote(send.at[others], land.at[others], send_sem, recv_sem, {"seq": 0})
    copy.wait_recv()
    return copy


def pack_rows(block_of, halves, send, column, width):
    parts = [block_of(h).T.reshape(width // GROUP, GROUP, LANES) for h in range(halves)]
    send[pl.ds(column // GROUP, width // GROUP)] = jnp.concatenate(parts, axis=1).astype(send.dtype)


def unpack_channels(land, wide, out):
    wide[...] = land[...].astype(jnp.float32).reshape(wide.shape)
    blocks = out.shape[1]
    for j in range(GROUP):
        out[j] = wide[pl.ds(j, blocks, stride=GROUP), :]


def front_kernel(
    branches, taps, gain, long_filter, weight,
    gate_out, direct_out, signal_out, filter_out, weight_a_out, weight_b_out,
    halo, extended, send_f, send_s, land_f, land_s, wide, weight_a, weight_b,
    halo_sems, a2a_sems, y_sems, x_send, x_recv, z_send, z_recv,
):
    seq_size = land_f.shape[0]
    nz, nx, ny = ring_sizes(seq_size)
    z, x, y = place(seq_size)
    me = lax.axis_index("seq")
    rows, channels = long_filter.shape
    halves = rows // LANES
    width = min(LANES, channels)
    half_columns = weight_a.shape[-1]

    following = lax.rem(me + 1, seq_size)
    halo_copy = remote(
        branches.at[:, pl.ds(rows - 16, 16), :], halo, halo_sems.at[0], halo_sems.at[1], {"seq": following}
    )
    halo_copy.start()
    weight_a[x, y] = weight[:, :half_columns]
    weight_b[z, y] = weight[:, half_columns:]
    other_y = me + 1 - 2 * y
    y_a = remote(weight_a.at[x, y], weight_a.at[x, y], y_sems.at[0], y_sems.at[1], {"seq": other_y})
    y_b = remote(weight_b.at[z, y], weight_b.at[z, y], y_sems.at[2], y_sems.at[3], {"seq": other_y})
    y_a.start()
    y_b.start()

    for column in range(0, channels, width):
        pack_rows(
            lambda h: long_filter[h * LANES : (h + 1) * LANES, column : column + width],
            halves, send_f, column, width,
        )
    scatter_start(send_f, land_f, a2a_sems.at[0], a2a_sems.at[1])

    halo_copy.wait()
    first = me == 0
    for column in range(0, channels, width):
        span = slice(column, column + width)
        mixed = []
        for branch in range(3):
            before = halo[branch, :, span].astype(jnp.float32)
            extended[branch, 0:16, :] = jnp.where(first, 0.0, before)
            extended[branch, 16:, :] = branches[branch, :, span].astype(jnp.float32)
            total = taps[0, branch : branch + 1, span] * extended[branch, 16 : 16 + rows, :]
            for lag in (1, 2):
                total += taps[lag, branch : branch + 1, span] * extended[branch, 16 - lag : 16 - lag + rows, :]
            mixed.append(total)
        signal = mixed[1] * mixed[2]
        gate_out[:, span] = mixed[0]
        direct_out[:, span] = gain[0:1, span] * signal
        pack_rows(lambda h: signal[h * LANES : (h + 1) * LANES], halves, send_s, column, width)
    scatter_start(send_s, land_s, a2a_sems.at[2], a2a_sems.at[3])

    y_a.wait()
    y_b.wait()
    x_copies = []
    for t in range(1, nx):
        peer_x = lax.rem(x + t, nx)
        copy = remote(
            weight_a.at[x], weight_a.at[x], x_send.at[t], x_recv.at[x], {"seq": (z * nx + peer_x) * ny + y}
        )
        copy.start()
        x_copies.append(copy)
    z_copies = []
    for t in range(1, nz):
        peer_z = lax.rem(z + t, nz)
        copy = remote(
            weight_b.at[z], weight_b.at[z], z_send.at[t], z_recv.at[z], {"seq": (peer_z * nx + x) * ny + y}
        )
        copy.start()
        z_copies.append(copy)

    copy_f = scatter_wait(send_f, land_f, a2a_sems.at[0], a2a_sems.at[1])
    unpack_channels(land_f, wide, filter_out)
    copy_s = scatter_wait(send_s, land_s, a2a_sems.at[2], a2a_sems.at[3])
    unpack_channels(land_s, wide, signal_out)
    for t in range(1, nx):
        source = lax.rem(x + nx - t, nx)
        remote(weight_a.at[source], weight_a.at[source], x_send.at[t], x_recv.at[source], {"seq": me}).wait_recv()
    for t in range(1, nz):
        source = lax.rem(z + nz - t, nz)
        remote(weight_b.at[source], weight_b.at[source], z_send.at[t], z_recv.at[source], {"seq": me}).wait_recv()
    weight_a_out[...] = weight_a[...]
    weight_b_out[...] = weight_b[...]
    copy_f.wait_send()
    copy_s.wait_send()
    for copy in x_copies + z_copies:
        copy.wait_send()


def convolve_kernel(scale, signal, long_filter, out, padded, taps, shifted, total, wide):
    blocks = signal.shape[1]
    step = min(2 * SHIFTS, blocks)
    padded[0:SHIFTS, :] = jnp.zeros((SHIFTS, LANES), jnp.float32)
    taps[0:8, :] = jnp.zeros((8, LANES), jnp.float32)
    row = lax.broadcasted_iota(jnp.int32, (LANES, LANES), 0)
    lane = lax.broadcasted_iota(jnp.int32, (LANES, LANES), 1)
    causal = lane >= row

    def rolled(block):
        line = jnp.broadcast_to(taps[8 + block : 9 + block, :], (LANES, LANES))
        return pltpu.roll(line, 0, 1, stride=1, stride_axis=0)

    def channel(j, carry):
        padded[SHIFTS:, :] = signal[j]
        taps[8:, :] = long_filter[j]
        for shift in range(SHIFTS):
            shifted[:, shift * LANES : (shift + 1) * LANES] = padded[
                SHIFTS - shift : SHIFTS - shift + blocks, :
            ].astype(jnp.bfloat16)
        for start in range(0, blocks, step):
            height = blocks - start
            spans = range(start, min(start + step, blocks), SHIFTS)
            last = [rolled(span - 1) for span in spans]
            partial = None
            for shift in range(0, SHIFTS, 2):
                tiles = []
                for extra in range(2):
                    here = [rolled(span + shift + extra) for span in spans]
                    tiles.append(
                        jnp.concatenate(
                            [jnp.where(causal, h, b).astype(jnp.bfloat16) for h, b in zip(here, last)], axis=1
                        )
                    )
                    last = here
                term = jnp.dot(
                    shifted[0:height, shift * LANES : (shift + 2) * LANES],
                    jnp.concatenate(tiles, axis=0),
                    preferred_element_type=jnp.float32,
                )
                partial = term if partial is None else partial + term
            if start == 0:
                total[...] = partial[:, :LANES]
            else:
                total[start:, :] += partial[:, :LANES]
            if len(spans) > 1:
                total[start + SHIFTS :, :] += partial[: height - SHIFTS, LANES:]
        wide[:, pl.ds(j, 1), :] = (total[...] * scale).reshape(blocks, 1, LANES)
        return carry

    lax.fori_loop(0, GROUP, channel, 0)
    out[...] = wide[...].reshape(out.shape).astype(out.dtype)


def back_kernel(
    convolved, gate, direct, weight_a_in, weight_b_in, out,
    land, gathered, weight_a, weight_b, total,
    a2a_sems, ring_send, ring_recv, x_send, x_recv, tp_send, near_send, tp_recv,
):
    seq_size = land.shape[0]
    nz, nx, ny = ring_sizes(seq_size)
    z, x, y = place(seq_size)
    me = lax.axis_index("seq")
    mine = lax.axis_index("tp")
    tp_size = gathered.shape[0]
    chips = tp_size // 2
    chip, core = mine // 2, mine % 2
    sibling = mine + 1 - 2 * core
    rows, channels = gate.shape
    halves = rows // LANES
    width = min(LANES, channels)

    scatter_start(convolved, land, a2a_sems.at[0], a2a_sems.at[1])
    weight_a[z] = weight_a_in[...]
    weight_b[x] = weight_b_in[...]
    forth = (lax.rem(z + 1, nz) * nx + x) * ny + y
    back = (lax.rem(z + nz - 1, nz) * nx + x) * ny + y
    middle = nx // 2

    def ring_copies(t):
        pair = []
        for way, peer in enumerate((forth, back)):
            block = lax.rem(z + nz - (t - 1), nz) if way == 0 else lax.rem(z + (t - 1), nz)
            piece = weight_a.at[block]
            if 2 * t == nz:
                piece = weight_a.at[block, pl.ds(way * middle, middle)]
            pair.append(remote(piece, piece, ring_send.at[way, t], ring_recv.at[way, t], {"seq": peer}))
        return pair

    ring = {t: ring_copies(t) for t in range(1, nz // 2 + 1)}

    def ring_start(t):
        for copy in ring[t]:
            copy.start()

    def ring_wait(t):
        for copy in ring[t]:
            copy.wait_recv()

    ring_start(1)
    x_copies = []
    for t in range(1, nx):
        peer_x = lax.rem(x + t, nx)
        copy = remote(
            weight_b.at[x], weight_b.at[x], x_send.at[t], x_recv.at[x], {"seq": (z * nx + peer_x) * ny + y}
        )
        copy.start()
        x_copies.append(copy)

    back_copy = scatter_wait(convolved, land, a2a_sems.at[0], a2a_sems.at[1])
    for column in range(0, channels, width):
        slots = pl.ds(column // GROUP, width // GROUP)
        arrived = land[slots].astype(jnp.float32)
        for h in range(halves):
            block = arrived[:, h * GROUP : (h + 1) * GROUP, :].reshape(width, LANES).T
            span = (slice(h * LANES, (h + 1) * LANES), slice(column, column + width))
            gated = gate[span] * (block + direct[span])
            gathered[mine, h * LANES : (h + 1) * LANES, column : column + width] = gated.astype(gathered.dtype)

    own = gathered.at[mine]
    tp_copies = [remote(own, own, near_send.at[0], tp_recv.at[mine], {"tp": sibling})]
    for t in range(1, chips):
        peer = lax.rem(chip + t, chips) * 2 + core
        tp_copies.append(remote(own, own, tp_send.at[t], tp_recv.at[mine], {"tp": peer}))
    for copy in tp_copies:
        copy.start()
    if nz // 2 >= 2:
        ring_wait(1)
        ring_start(2)
    for t in range(1, chips):
        source = lax.rem(chip + chips - t, chips) * 2 + core
        slot = gathered.at[source]
        copy = remote(slot, slot, near_send.at[t], tp_recv.at[source], {"tp": sibling})
        copy.wait_recv()
        copy.start()
        tp_copies.append(copy)
        if t + 2 <= nz // 2:
            ring_wait(t + 1)
            ring_start(t + 2)
    for t in range(0, chips):
        source = lax.rem(chip + chips - t, chips) * 2 + 1 - core
        slot = gathered.at[source]
        remote(slot, slot, near_send.at[t], tp_recv.at[source], {"tp": sibling}).wait_recv()
    ring_wait(nz // 2)
    for t in range(1, nx):
        source = lax.rem(x + nx - t, nx)
        remote(weight_b.at[source], weight_b.at[source], x_send.at[t], x_recv.at[source], {"seq": me}).wait_recv()

    columns = weight_a.shape[-1]
    for part in range(2):
        total[...] = jnp.zeros_like(total)

        def add(block, carry):
            tile = weight_a[block] if part == 0 else weight_b[:, block]
            total[...] += jnp.dot(
                gathered[block], tile.reshape(channels, columns), preferred_element_type=jnp.float32
            )
            return carry

        lax.fori_loop(0, tp_size, add, 0)
        out[:, part * columns : (part + 1) * columns] = total[...].astype(out.dtype)

    back_copy.wait_send()
    for t in ring:
        for copy in ring[t]:
            copy.wait_send()
    for copy in x_copies + tp_copies:
        copy.wait_send()


def vmem(count):
    return [pl.BlockSpec(memory_space=pltpu.VMEM)] * count


def body(seq_size, tp_size, branches, short_taps, skip_gain, long_filter, out_weight):
    rows, channels = long_filter.shape
    weight_rows, columns = out_weight.shape
    nz, nx, ny = ring_sizes(seq_size)
    assert channels == GROUP * seq_size and nz == tp_size and nx * ny * weight_rows == channels
    halves = rows // LANES
    blocks = halves * seq_size
    half = columns // 2
    slots = (seq_size, halves * GROUP, LANES)
    f32, b16 = jnp.float32, jnp.bfloat16
    dma = pltpu.SemaphoreType.DMA
    shape = jax.ShapeDtypeStruct

    gate, direct, signal, filters, weight_a, weight_b = pl.pallas_call(
        front_kernel,
        out_shape=[
            shape((rows, channels), f32),
            shape((rows, channels), f32),
            shape((GROUP, blocks, LANES), f32),
            shape((GROUP, blocks, LANES), f32),
            shape((nx, ny, weight_rows, half), b16),
            shape((nz, ny, weight_rows, half), b16),
        ],
        in_specs=vmem(5),
        out_specs=vmem(6),
        scratch_shapes=[
            pltpu.VMEM((3, 16, channels), b16),
            pltpu.VMEM((3, 16 + rows, min(LANES, channels)), f32),
            pltpu.VMEM(slots, b16),
            pltpu.VMEM(slots, b16),
            pltpu.VMEM(slots, b16),
            pltpu.VMEM(slots, b16),
            pltpu.VMEM((blocks * GROUP, LANES), f32),
            pltpu.VMEM((nx, ny, weight_rows, half), b16),
            pltpu.VMEM((nz, ny, weight_rows, half), b16),
            dma((2,)),
            dma((4,)),
            dma((4,)),
            dma((nx,)),
            dma((nx,)),
            dma((nz,)),
            dma((nz,)),
        ],
        compiler_params=pltpu.CompilerParams(has_side_effects=True, vmem_limit_bytes=32 << 20),
        name="front",
    )(branches, short_taps, skip_gain[None, :], long_filter, out_weight)

    scale = 1.0 / math.sqrt(float(rows * seq_size))
    convolved = pl.pallas_call(
        functools.partial(convolve_kernel, scale),
        out_shape=shape(slots, b16),
        in_specs=vmem(2),
        out_specs=vmem(1)[0],
        scratch_shapes=[
            pltpu.VMEM((SHIFTS + blocks, LANES), f32),
            pltpu.VMEM((8 + blocks, LANES), f32),
            pltpu.VMEM((blocks, SHIFTS * LANES), b16),
            pltpu.VMEM((blocks, LANES), f32),
            pltpu.VMEM((blocks, GROUP, LANES), f32),
        ],
        compiler_params=pltpu.CompilerParams(vmem_limit_bytes=32 << 20),
        name="convolve",
    )(signal, filters)

    steps = nz // 2 + 1
    chips = tp_size // 2
    return pl.pallas_call(
        back_kernel,
        out_shape=shape((rows, columns), b16),
        in_specs=vmem(5),
        out_specs=vmem(1)[0],
        scratch_shapes=[
            pltpu.VMEM(slots, b16),
            pltpu.VMEM((tp_size, rows, channels), b16),
            pltpu.VMEM((nz, nx, ny, weight_rows, half), b16),
            pltpu.VMEM((nx, nz, ny, weight_rows, half), b16),
            pltpu.VMEM((rows, half), f32),
            dma((2,)),
            dma((2, steps)),
            dma((2, steps)),
            dma((nx,)),
            dma((nx,)),
            dma((chips,)),
            dma((chips,)),
            dma((tp_size,)),
        ],
        compiler_params=pltpu.CompilerParams(has_side_effects=True, vmem_limit_bytes=32 << 20),
        name="back",
    )(convolved, gate, direct, weight_a, weight_b)


def solution(mesh):
    in_specs = (P(None, "seq", "tp"), P(None, None, "tp"), P("tp"), P("seq", "tp"), P("seq", "tp"))
    return jax.shard_map(
        functools.partial(body, mesh.shape["seq"], mesh.shape["tp"]),
        mesh=mesh,
        in_specs=in_specs,
        out_specs=P("seq", "tp"),
        check_vma=False,
    )
```

```python
import functools
import math

import jax
import jax.numpy as jnp
from jax import lax
from jax.experimental import pallas as pl
from jax.experimental.pallas import tpu as pltpu
from jax.sharding import PartitionSpec as P

MESH = pl.DeviceIdType.MESH
LANES = 128
GROUP = 8
SHIFTS = 16


def ring_sizes(seq_size):
    return (seq_size // 8, 4, 2) if seq_size >= 32 else (seq_size // 4, 2, 2)


def place(seq_size):
    nz, nx, ny = ring_sizes(seq_size)
    me = lax.axis_index("seq")
    return me // (nx * ny), (me // ny) % nx, me % ny


def remote(src, dst, send_sem, recv_sem, device_id):
    return pltpu.make_async_remote_copy(
        src_ref=src,
        dst_ref=dst,
        send_sem=send_sem,
        recv_sem=recv_sem,
        device_id=device_id,
        device_id_type=MESH,
    )


def scatter_start(send, land, send_sem, recv_sem):
    count = send.shape[0]
    me = lax.axis_index("seq")

    def step(t, carry):
        peer = lax.rem(me + t, count)
        remote(send.at[peer], land.at[me], send_sem, recv_sem, {"seq": peer}).start()
        return carry

    lax.fori_loop(1, count, step, 0)
    land[me] = send[me]


def scatter_wait(send, land, send_sem, recv_sem):
    others = pl.ds(0, send.shape[0] - 1)
    copy = remote(send.at[others], land.at[others], send_sem, recv_sem, {"seq": 0})
    copy.wait_recv()
    return copy


def pack_rows(block_of, halves, send, column, width):
    parts = [block_of(h).T.reshape(width // GROUP, GROUP, LANES) for h in range(halves)]
    send[pl.ds(column // GROUP, width // GROUP)] = jnp.concatenate(parts, axis=1).astype(send.dtype)


def unpack_channels(land, wide, out):
    wide[...] = land[...].astype(jnp.float32).reshape(wide.shape)
    blocks = out.shape[1]
    for j in range(GROUP):
        out[j] = wide[pl.ds(j, blocks, stride=GROUP), :]


def block_kernel(
    scale, branches, taps, gain, long_filter, weight, out,
    halo, extended, send_f, send_s, land_f, land_s, land_b, wide, gate, direct, signal, filters,
    padded, filter_rows, shifted, total, first_a, first_b, weight_a, weight_b, gathered, product,
    round_sems, halo_sems, a2a_sems, y_sems, xa_send, xa_recv, zb_send, zb_recv,
    ring_send, ring_recv, xb_send, xb_recv, tp_send, tp_recv,
):
    seq_size, tp_size = land_f.shape[0], gathered.shape[0]
    nz, nx, ny = ring_sizes(seq_size)
    z, x, y = place(seq_size)
    me, mine = lax.axis_index("seq"), lax.axis_index("tp")
    rows, channels = long_filter.shape
    halves = rows // LANES
    width = min(LANES, channels)
    half_columns = first_a.shape[-1]

    def at(z, x, y):
        return {"seq": (z * nx + x) * ny + y}

    x_peers = [at(z, lax.rem(x + t, nx), y) for t in range(1, nx)]
    z_peers = [at(lax.rem(z + t, nz), x, y) for t in range(1, nz)]
    tp_peers = [{"tp": lax.rem(mine + t, tp_size)} for t in range(1, tp_size)]
    other_y = at(z, x, 1 - y)
    following = {"seq": lax.rem(me + 1, seq_size)}
    leading = {"seq": lax.rem(me + seq_size - 1, seq_size)}

    barrier = pltpu.get_barrier_semaphore()
    greeted = [other_y, following, leading] + x_peers + z_peers + tp_peers
    for peer in greeted:
        pl.semaphore_signal(barrier, inc=1, device_id=peer, device_id_type=MESH)
    first_a[x, y] = weight[:, :half_columns]
    first_b[z, y] = weight[:, half_columns:]
    for column in range(0, channels, width):
        pack_rows(
            lambda h: long_filter[h * LANES : (h + 1) * LANES, column : column + width],
            halves, send_f, column, width,
        )
    pl.semaphore_wait(barrier, len(greeted))
    for peer in x_peers:
        pl.semaphore_signal(round_sems.at[0], inc=1, device_id=peer, device_id_type=MESH)
    halo_copy = remote(
        branches.at[:, pl.ds(rows - 16, 16), :], halo, halo_sems.at[0], halo_sems.at[1], following
    )
    halo_copy.start()
    y_a = remote(first_a.at[x, y], first_a.at[x, y], y_sems.at[0], y_sems.at[1], other_y)
    y_b = remote(first_b.at[z, y], first_b.at[z, y], y_sems.at[2], y_sems.at[3], other_y)
    y_a.start()
    y_b.start()
    pl.semaphore_wait(round_sems.at[0], nx - 1)
    pl.semaphore_signal(round_sems.at[1], inc=1, device_id=other_y, device_id_type=MESH)
    pl.semaphore_wait(round_sems.at[1], 1)

    scatter_start(send_f, land_f, a2a_sems.at[0], a2a_sems.at[1])
    halo_copy.wait()
    first = me == 0
    for column in range(0, channels, width):
        span = slice(column, column + width)
        mixed = []
        for branch in range(3):
            before = halo[branch, :, span].astype(jnp.float32)
            extended[branch, 0:16, :] = jnp.where(first, 0.0, before)
            extended[branch, 16:, :] = branches[branch, :, span].astype(jnp.float32)
            mix = taps[0, branch : branch + 1, span] * extended[branch, 16 : 16 + rows, :]
            for lag in (1, 2):
                mix += taps[lag, branch : branch + 1, span] * extended[branch, 16 - lag : 16 - lag + rows, :]
            mixed.append(mix)
        made = mixed[1] * mixed[2]
        gate[:, span] = mixed[0]
        direct[:, span] = gain[0:1, span] * made
        pack_rows(lambda h: made[h * LANES : (h + 1) * LANES], halves, send_s, column, width)
    scatter_start(send_s, land_s, a2a_sems.at[2], a2a_sems.at[3])
    y_a.wait()
    y_b.wait()
    copy_f = scatter_wait(send_f, land_f, a2a_sems.at[0], a2a_sems.at[1])
    unpack_channels(land_f, wide, filters)
    copy_s = scatter_wait(send_s, land_s, a2a_sems.at[2], a2a_sems.at[3])

    sent = [copy_f]
    for t, peer in enumerate(x_peers):
        sent.append(remote(first_a.at[x], first_a.at[x], xa_send.at[t], xa_recv.at[x], peer))
    for t, peer in enumerate(z_peers):
        sent.append(remote(first_b.at[z], first_b.at[z], zb_send.at[t], zb_recv.at[z], peer))
    for copy in sent[1:]:
        copy.start()
    unpack_channels(land_s, wide, signal)

    ring_peers = at(lax.rem(z + 1, nz), x, y), at(lax.rem(z + nz - 1, nz), x, y)
    middle = nx // 2

    def ring_copy(way, t):
        block = lax.rem(z + nz - (t - 1), nz) if way == 0 else lax.rem(z + (t - 1), nz)
        piece = weight_a.at[block]
        if 2 * t == nz:
            piece = weight_a.at[block, pl.ds(way * middle, middle)]
        return remote(piece, piece, ring_send.at[way, t], ring_recv.at[way, t], ring_peers[way])

    def ring_start(t):
        for way in range(2):
            ring_copy(way, t).start()

    def ring_wait(t):
        for way in range(2):
            ring_copy(way, t).wait_recv()

    def first_ring():
        for t in range(1, nx):
            source = lax.rem(x + nx - t, nx)
            remote(first_a.at[source], first_a.at[source], xa_send.at[t], xa_recv.at[source], other_y).wait_recv()
        weight_a[z] = first_a[...]
        ring_start(1)

    convolve(scale, signal, filters, padded, filter_rows, shifted, total, wide, first_ring)
    copy_s.wait_send()
    send_s[...] = wide[...].reshape(send_s.shape).astype(send_s.dtype)
    scatter_start(send_s, land_b, a2a_sems.at[4], a2a_sems.at[5])
    for t in range(1, nz):
        source = lax.rem(z + nz - t, nz)
        remote(first_b.at[source], first_b.at[source], zb_send.at[0], zb_recv.at[source], other_y).wait_recv()
    weight_b[x] = first_b[...]
    for t, peer in enumerate(x_peers):
        copy = remote(weight_b.at[x], weight_b.at[x], xb_send.at[t], xb_recv.at[x], peer)
        copy.start()
        sent.append(copy)
    ring_wait(1)
    if nz // 2 >= 2:
        ring_start(2)
    sent.append(scatter_wait(send_s, land_b, a2a_sems.at[4], a2a_sems.at[5]))

    for column in range(0, channels, width):
        slots = pl.ds(column // GROUP, width // GROUP)
        arrived = land_b[slots].astype(jnp.float32)
        for h in range(halves):
            block = arrived[:, h * GROUP : (h + 1) * GROUP, :].reshape(width, LANES).T
            span = (slice(h * LANES, (h + 1) * LANES), slice(column, column + width))
            gated = gate[span] * (block + direct[span])
            gathered[mine, h * LANES : (h + 1) * LANES, column : column + width] = gated.astype(gathered.dtype)
    chips = tp_size // 2
    chip, core = mine // 2, lax.rem(mine, 2)

    def tp_copy(slot, kind, to):
        return remote(gathered.at[slot], gathered.at[slot], tp_send.at[kind, slot], tp_recv.at[slot], {"tp": to})

    def up(slot):
        return tp_copy(slot, 0, mine + 2)

    def down(slot):
        return tp_copy(slot, 1, mine - 2)

    def side(slot):
        return tp_copy(slot, 2, mine + 1 - 2 * core)

    pl.when(chip < chips - 1)(lambda: up(mine).start())
    pl.when(chip > 0)(lambda: down(mine).start())
    side(mine).start()
    for t in range(1, chips):
        if t + 2 <= nz // 2:
            ring_wait(t + 1)
            ring_start(t + 2)

        @pl.when(chip >= t)
        def _():
            slot = mine - 2 * t
            side(slot).wait_recv()
            pl.when(chip < chips - 1)(lambda: up(slot).start())
            side(slot).start()

        @pl.when(chip + t < chips)
        def _():
            slot = mine + 2 * t
            side(slot).wait_recv()
            pl.when(chip > 0)(lambda: down(slot).start())
            side(slot).start()

    for k in range(chips):
        side(2 * k + 1 - core).wait_recv()
    if nz // 2 >= 2:
        ring_wait(nz // 2)
    for t in range(1, nx):
        source = lax.rem(x + nx - t, nx)
        remote(weight_b.at[source], weight_b.at[source], xb_send.at[0], xb_recv.at[source], other_y).wait_recv()

    for part in range(2):
        product[...] = jnp.zeros_like(product)

        def add(block, carry):
            tile = weight_a[block] if part == 0 else weight_b[:, block]
            product[...] += jnp.dot(
                gathered[block], tile.reshape(channels, half_columns), preferred_element_type=jnp.float32
            )
            return carry

        lax.fori_loop(0, tp_size, add, 0)
        out[:, part * half_columns : (part + 1) * half_columns] = product[...].astype(out.dtype)

    for copy in sent:
        copy.wait_send()
    for t in range(1, nz // 2 + 1):
        for way in range(2):
            ring_copy(way, t).wait_send()
    for k in range(chips):
        slot = 2 * k + core
        side(slot).wait_send()
        pl.when((k <= chip) & (chip < chips - 1))(lambda: up(slot).wait_send())
        pl.when((k >= chip) & (chip > 0))(lambda: down(slot).wait_send())


def convolve(scale, signal, long_filter, padded, taps, shifted, total, wide, midway):
    blocks = signal.shape[1]
    step = min(2 * SHIFTS, blocks)
    padded[0:SHIFTS, :] = jnp.zeros((SHIFTS, LANES), jnp.float32)
    taps[0:8, :] = jnp.zeros((8, LANES), jnp.float32)
    row = lax.broadcasted_iota(jnp.int32, (LANES, LANES), 0)
    lane = lax.broadcasted_iota(jnp.int32, (LANES, LANES), 1)
    causal = lane >= row

    def rolled(block):
        line = jnp.broadcast_to(taps[8 + block : 9 + block, :], (LANES, LANES))
        return pltpu.roll(line, 0, 1, stride=1, stride_axis=0)

    def channel(j, carry):
        pl.when(j == GROUP // 2)(midway)
        padded[SHIFTS:, :] = signal[j]
        taps[8:, :] = long_filter[j]
        for shift in range(SHIFTS):
            shifted[:, shift * LANES : (shift + 1) * LANES] = padded[
                SHIFTS - shift : SHIFTS - shift + blocks, :
            ].astype(jnp.bfloat16)
        for start in range(0, blocks, step):
            height = blocks - start
            spans = range(start, min(start + step, blocks), SHIFTS)
            last = [rolled(span - 1) for span in spans]
            partial = None
            for shift in range(0, SHIFTS, 2):
                tiles = []
                for extra in range(2):
                    here = [rolled(span + shift + extra) for span in spans]
                    tiles.append(
                        jnp.concatenate(
                            [jnp.where(causal, h, b).astype(jnp.bfloat16) for h, b in zip(here, last)], axis=1
                        )
                    )
                    last = here
                term = jnp.dot(
                    shifted[0:height, shift * LANES : (shift + 2) * LANES],
                    jnp.concatenate(tiles, axis=0),
                    preferred_element_type=jnp.float32,
                )
                partial = term if partial is None else partial + term
            if start == 0:
                total[...] = partial[:, :LANES]
            else:
                total[start:, :] += partial[:, :LANES]
            if len(spans) > 1:
                total[start + SHIFTS :, :] += partial[: height - SHIFTS, LANES:]
        wide[pl.ds(j, blocks, stride=GROUP), :] = total[...] * scale
        return carry

    lax.fori_loop(0, GROUP, channel, 0)


def body(seq_size, tp_size, branches, short_taps, skip_gain, long_filter, out_weight):
    rows, channels = long_filter.shape
    weight_rows, columns = out_weight.shape
    nz, nx, ny = ring_sizes(seq_size)
    assert channels == GROUP * seq_size and nz == tp_size and nx * ny * weight_rows == channels
    halves = rows // LANES
    blocks = halves * seq_size
    half = columns // 2
    slots = (seq_size, halves * GROUP, LANES)
    f32, b16 = jnp.float32, jnp.bfloat16
    dma = pltpu.SemaphoreType.DMA
    steps = nz // 2 + 1
    scale = 1.0 / math.sqrt(float(rows * seq_size))
    return pl.pallas_call(
        functools.partial(block_kernel, scale),
        out_shape=jax.ShapeDtypeStruct((rows, columns), b16),
        in_specs=[pl.BlockSpec(memory_space=pltpu.VMEM)] * 5,
        out_specs=pl.BlockSpec(memory_space=pltpu.VMEM),
        scratch_shapes=[
            pltpu.VMEM((3, 16, channels), b16),
            pltpu.VMEM((3, 16 + rows, min(LANES, channels)), f32),
            *[pltpu.VMEM(slots, b16)] * 5,
            pltpu.VMEM((blocks * GROUP, LANES), f32),
            *[pltpu.VMEM((rows, channels), f32)] * 2,
            *[pltpu.VMEM((GROUP, blocks, LANES), f32)] * 2,
            pltpu.VMEM((SHIFTS + blocks, LANES), f32),
            pltpu.VMEM((8 + blocks, LANES), f32),
            pltpu.VMEM((blocks, SHIFTS * LANES), b16),
            pltpu.VMEM((blocks, LANES), f32),
            pltpu.VMEM((nx, ny, weight_rows, half), b16),
            pltpu.VMEM((nz, ny, weight_rows, half), b16),
            pltpu.VMEM((nz, nx, ny, weight_rows, half), b16),
            pltpu.VMEM((nx, nz, ny, weight_rows, half), b16),
            pltpu.VMEM((tp_size, rows, channels), b16),
            pltpu.VMEM((rows, half), f32),
            pltpu.SemaphoreType.REGULAR((2,)),
            dma((2,)),
            dma((6,)),
            dma((4,)),
            dma((nx,)),
            dma((nx,)),
            dma((nz,)),
            dma((nz,)),
            dma((2, steps)),
            dma((2, steps)),
            dma((nx,)),
            dma((nx,)),
            dma((3, tp_size)),
            dma((tp_size,)),
        ],
        compiler_params=pltpu.CompilerParams(has_side_effects=True, collective_id=0, vmem_limit_bytes=40 << 20),
        name="hyena",
    )(branches, short_taps, skip_gain[None, :], long_filter, out_weight)


def solution(mesh):
    in_specs = (P(None, "seq", "tp"), P(None, None, "tp"), P("tp"), P("seq", "tp"), P("seq", "tp"))
    return jax.shard_map(
        functools.partial(body, mesh.shape["seq"], mesh.shape["tp"]),
        mesh=mesh,
        in_specs=in_specs,
        out_specs=P("seq", "tp"),
        check_vma=False,
    )
```

```python
import functools
import math

import jax
import jax.numpy as jnp
from jax import lax
from jax.experimental import pallas as pl
from jax.experimental.pallas import tpu as pltpu
from jax.sharding import PartitionSpec as P

MESH = pl.DeviceIdType.MESH
LANES = 128
GROUP = 8
SHIFTS = 16
SCHEDULE = {
    "halo": ("y", "as"),
    "sent": ("b1",),
    "filter": ("b2",),
    "signal": ("b3", "n0", "n1", "a1"),
    1: ("b4", "n2"),
    3: ("b5", "n3", "n4", "a2"),
    5: ("a3",),
    "gated": ("bl", "a4"),
    "passed 3": ("a5", "bd"),
}


def ring_sizes(seq_size):
    return (seq_size // 8, 4, 2) if seq_size >= 32 else (seq_size // 4, 2, 2)


def place(seq_size):
    nz, nx, ny = ring_sizes(seq_size)
    me = lax.axis_index("seq")
    return me // (nx * ny), (me // ny) % nx, me % ny


def remote(src, dst, send_sem, recv_sem, device_id):
    return pltpu.make_async_remote_copy(
        src_ref=src,
        dst_ref=dst,
        send_sem=send_sem,
        recv_sem=recv_sem,
        device_id=device_id,
        device_id_type=MESH,
    )


def scatter_start(send, land, send_sem, recv_sem):
    count = send.shape[0]
    me = lax.axis_index("seq")

    def step(t, carry):
        peer = lax.rem(me + t, count)
        remote(send.at[peer], land.at[me], send_sem, recv_sem, {"seq": peer}).start()
        return carry

    lax.fori_loop(1, count, step, 0)
    land[me] = send[me]


def scatter_wait(send, land, send_sem, recv_sem):
    others = pl.ds(0, send.shape[0] - 1)
    copy = remote(send.at[others], land.at[others], send_sem, recv_sem, {"seq": 0})
    copy.wait_recv()
    return copy


def pack_rows(block_of, halves, send, column, width):
    parts = [block_of(h).T.reshape(width // GROUP, GROUP, LANES) for h in range(halves)]
    send[pl.ds(column // GROUP, width // GROUP)] = jnp.concatenate(parts, axis=1).astype(send.dtype)


def unpack_channels(land, wide, out):
    wide[...] = land[...].astype(jnp.float32).reshape(wide.shape)
    blocks = out.shape[1]
    for j in range(GROUP):
        out[j] = wide[pl.ds(j, blocks, stride=GROUP), :]


def block_kernel(
    scale, branches, taps, gain, long_filter, weight, out,
    halo, extended, send_f, send_s, land_f, land_s, land_b, wide, gate, direct, signal, filters,
    padded, filter_rows, shifted, total, weight_a, weight_b, gathered, product,
    round_sems, halo_sems, a2a_sems, y_sems, xa_send, xa_recv, za_send, za_recv, zb_send, zb_recv,
    xb_send, xb_recv, far_send, far_recv, back_recv, tp_send, tp_recv,
):
    seq_size, tp_size = land_f.shape[0], gathered.shape[0]
    nz, nx, ny = ring_sizes(seq_size)
    z, x, y = place(seq_size)
    me, mine = lax.axis_index("seq"), lax.axis_index("tp")
    rows, channels = long_filter.shape
    halves = rows // LANES
    width = min(LANES, channels)
    columns_a = weight_a.shape[-1]

    def at(z, x, y):
        return {"seq": (z * nx + x) * ny + y}

    x_peers = [at(z, lax.rem(x + t, nx), y) for t in range(1, nx)]
    z_peers = [at(lax.rem(z + t, nz), x, y) for t in range(1, nz)]
    tp_peers = [{"tp": lax.rem(mine + t, tp_size)} for t in range(1, tp_size)]
    other_y = at(z, x, 1 - y)
    following = {"seq": lax.rem(me + 1, seq_size)}
    leading = {"seq": lax.rem(me + seq_size - 1, seq_size)}

    barrier = pltpu.get_barrier_semaphore()
    greeted = [other_y, following, leading] + x_peers + z_peers + tp_peers
    for peer in greeted:
        pl.semaphore_signal(barrier, inc=1, device_id=peer, device_id_type=MESH)
    weight_a[z, x, y] = weight[:, :columns_a]
    weight_b[x, z, y] = weight[:, columns_a:]
    for column in range(0, channels, width):
        pack_rows(
            lambda h: long_filter[h * LANES : (h + 1) * LANES, column : column + width],
            halves, send_f, column, width,
        )
    pl.semaphore_wait(barrier, len(greeted))
    for peer in x_peers:
        pl.semaphore_signal(round_sems.at[0], inc=1, device_id=peer, device_id_type=MESH)
    halo_copy = remote(
        branches.at[:, pl.ds(rows - 16, 16), :], halo, halo_sems.at[0], halo_sems.at[1], following
    )
    halo_copy.start()
    y_a = remote(weight_a.at[z, x, y], weight_a.at[z, x, y], y_sems.at[0], y_sems.at[1], other_y)
    y_b = remote(weight_b.at[x, z, y], weight_b.at[x, z, y], y_sems.at[2], y_sems.at[3], other_y)
    y_a.start()
    y_b.start()
    pl.semaphore_wait(round_sems.at[0], nx - 1)
    pl.semaphore_signal(round_sems.at[1], inc=1, device_id=other_y, device_id_type=MESH)
    pl.semaphore_wait(round_sems.at[1], 1)

    sent = []
    z_pair = at(lax.rem(z + 1, nz), x, y), at(lax.rem(z + nz - 1, nz), x, y)
    x_pair = at(z, lax.rem(x + 1, nx), y), at(z, lax.rem(x + nx - 1, nx), y)

    def z_block(way, t):
        return lax.rem(z + nz - t, nz) if way == 0 else lax.rem(z + t, nz)

    def a_ring(way, t):
        block = z_block(way, t - 1)
        piece = weight_a.at[block, pl.ds(way * (nx // 2), nx // 2)] if 2 * t == nz else weight_a.at[block]
        return remote(piece, piece, za_send.at[way, t], za_recv.at[way, t], z_pair[way])

    def b_ring(way, t):
        block = z_block(way, t - 1)
        piece = weight_b.at[x, block, way] if 2 * t == nz else weight_b.at[x, block]
        return remote(piece, piece, zb_send.at[way, t], zb_recv.at[way, t], z_pair[way])

    def b_next(way, block):
        piece = weight_b.at[x, block]
        return remote(piece, piece, xb_send.at[way, block], xb_recv.at[way, block], x_pair[way])

    def b_far(way):
        source = lax.rem(x + nx - 1, nx) if way == 0 else lax.rem(x + 1, nx)
        piece = weight_b.at[source, pl.ds(way * (nz // 2), nz // 2)]
        return remote(piece, piece, far_send.at[way], far_recv.at[way], x_pair[way])

    def y_done():
        y_a.wait()
        y_b.wait()

    def a_spread():
        for t, peer in enumerate(x_peers):
            copy = remote(weight_a.at[z, x], weight_a.at[z, x], xa_send.at[t], xa_recv.at[x], peer)
            copy.start()
            sent.append(copy)

    def a_step(t):
        if t == 1:
            for i in range(1, nx):
                source = lax.rem(x + nx - i, nx)
                arrived = weight_a.at[z, source]
                remote(arrived, arrived, xa_send.at[0], xa_recv.at[source], other_y).wait_recv()
        for way in range(2):
            if t > 1:
                a_ring(way, t - 1).wait_recv()
        for way in range(2):
            if 2 * t <= nz:
                a_ring(way, t).start()

    def b_step(t):
        for way in range(2):
            if t > 1:
                b_ring(way, t - 1).wait_recv()
        for way in range(2):
            if 2 * t <= nz:
                b_ring(way, t).start()

    def b_along(t):
        for block in [z_block(0, t)] if t == 0 or 2 * t == nz else [z_block(0, t), z_block(1, t)]:
            for way in range(2):
                b_next(way, block).start()

    def b_last():
        for way in range(2):
            for block in range(nz):
                b_next(way, block).wait_recv()
        for way in range(2):
            b_far(way).start()

    def b_done():
        for way in range(2):
            b_far(way).wait_recv()

    steps = {"y": y_done, "as": a_spread, "bl": b_last, "bd": b_done}
    for t in range(1, nz // 2 + 2):
        steps[f"a{t}"] = functools.partial(a_step, t)
        steps[f"b{t}"] = functools.partial(b_step, t)
        steps[f"n{t - 1}"] = functools.partial(b_along, t - 1)

    def weight_steps(point):
        for name in SCHEDULE.get(point, ()):
            steps[name]()

    def pump(j):
        for channel in range(GROUP):
            if channel in SCHEDULE:
                pl.when(j == channel)(functools.partial(weight_steps, channel))

    scatter_start(send_f, land_f, a2a_sems.at[0], a2a_sems.at[1])
    halo_copy.wait()
    weight_steps("halo")
    first = me == 0
    for column in range(0, channels, width):
        span = slice(column, column + width)
        mixed = []
        for branch in range(3):
            before = halo[branch, :, span].astype(jnp.float32)
            extended[branch, 0:16, :] = jnp.where(first, 0.0, before)
            extended[branch, 16:, :] = branches[branch, :, span].astype(jnp.float32)
            mix = taps[0, branch : branch + 1, span] * extended[branch, 16 : 16 + rows, :]
            for lag in (1, 2):
                mix += taps[lag, branch : branch + 1, span] * extended[branch, 16 - lag : 16 - lag + rows, :]
            mixed.append(mix)
        made = mixed[1] * mixed[2]
        gate[:, span] = mixed[0]
        direct[:, span] = gain[0:1, span] * made
        pack_rows(lambda h: made[h * LANES : (h + 1) * LANES], halves, send_s, column, width)
    scatter_start(send_s, land_s, a2a_sems.at[2], a2a_sems.at[3])
    weight_steps("sent")
    copy_f = scatter_wait(send_f, land_f, a2a_sems.at[0], a2a_sems.at[1])
    sent.append(copy_f)
    unpack_channels(land_f, wide, filters)
    weight_steps("filter")
    copy_s = scatter_wait(send_s, land_s, a2a_sems.at[2], a2a_sems.at[3])
    unpack_channels(land_s, wide, signal)
    weight_steps("signal")
    convolve(scale, signal, filters, padded, filter_rows, shifted, total, wide, pump)
    copy_s.wait_send()
    send_s[...] = wide[...].reshape(send_s.shape).astype(send_s.dtype)
    parts = tp_send.shape[2]
    per_part = seq_size // parts
    my_part = me // per_part

    def part_at(k):
        return lax.rem(my_part + parts - k, parts)

    for k in range(parts):

        def send_back(i, carry):
            peer = lax.rem(my_part + k, parts) * per_part + lax.rem(me + i, per_part)
            remote(send_s.at[peer], land_b.at[me], a2a_sems.at[4], back_recv.at[my_part], {"seq": peer}).start()
            return carry

        lax.fori_loop(1 if k == 0 else 0, per_part, send_back, 0)
    land_b[me] = send_s[me]
    sent.append(remote(send_s.at[pl.ds(1, seq_size - 1)], land_b.at[pl.ds(1, seq_size - 1)], a2a_sems.at[4], a2a_sems.at[5], other_y))
    weight_steps("back")

    chips = tp_size // 2
    chip, core = mine // 2, lax.rem(mine, 2)

    def tp_copy(slot, k, kind, to):
        piece = gathered.at[slot, :, pl.ds(pl.multiple_of(part_at(k) * width, width), width)]
        return remote(piece, piece, tp_send.at[kind, slot, k], tp_recv.at[slot, k], {"tp": to})

    def up(slot, k):
        return tp_copy(slot, k, 0, mine + 2)

    def down(slot, k):
        return tp_copy(slot, k, 1, mine - 2)

    def side(slot, k):
        return tp_copy(slot, k, 2, mine + 1 - 2 * core)

    for k in range(parts):
        part = part_at(k)
        landed = land_b.at[pl.ds(part * per_part, per_part - 1 if k == 0 else per_part)]
        remote(landed, landed, a2a_sems.at[4], back_recv.at[part], other_y).wait_recv()
        arrived = land_b[pl.ds(part * per_part, per_part)].astype(jnp.float32)
        columns = pl.ds(pl.multiple_of(part * width, width), width)
        for h in range(halves):
            block = arrived[:, h * GROUP : (h + 1) * GROUP, :].reshape(width, LANES).T
            span = (pl.ds(h * LANES, LANES), columns)
            gathered[mine, h * LANES : (h + 1) * LANES, columns] = (
                gate[span] * (block + direct[span])
            ).astype(gathered.dtype)
        pl.when(chip < chips - 1)(lambda: up(mine, k).start())
        pl.when(chip > 0)(lambda: down(mine, k).start())
        side(mine, k).start()
    weight_steps("gated")

    def pass_on(t):
        for k in range(parts):

            @pl.when(chip >= t)
            def _():
                slot = mine - 2 * t
                side(slot, k).wait_recv()
                pl.when(chip < chips - 1)(lambda: up(slot, k).start())
                side(slot, k).start()

            @pl.when(chip + t < chips)
            def _():
                slot = mine + 2 * t
                side(slot, k).wait_recv()
                pl.when(chip > 0)(lambda: down(slot, k).start())
                side(slot, k).start()

    def add(slot):
        for tile, span in (
            (weight_a[slot], slice(0, columns_a)),
            (weight_b[:, slot], slice(columns_a, columns_a + weight_b.shape[-1])),
        ):
            product[:, span] += jnp.dot(
                gathered[slot], tile.reshape(channels, tile.shape[-1]), preferred_element_type=jnp.float32
            )

    def add_pair(slot):
        other = slot + 1 - 2 * core
        for k in range(parts):
            side(other, k).wait_recv()
        add(slot)
        add(other)

    def add_all(t):
        pl.when(chip >= t)(lambda: add_pair(mine - 2 * t))
        if t > 0:
            pl.when(chip + t < chips)(lambda: add_pair(mine + 2 * t))

    product[...] = jnp.zeros_like(product)
    for t in range(1, chips):
        pass_on(t)
        weight_steps(f"passed {t}")
    for t in range(chips):
        add_all(t)
    out[...] = product[...].astype(out.dtype)

    for copy in sent:
        copy.wait_send()
    for way in range(2):
        for t in range(1, nz // 2 + 1):
            a_ring(way, t).wait_send()
            b_ring(way, t).wait_send()
        for block in range(nz):
            b_next(way, block).wait_send()
        b_far(way).wait_send()
    for i in range(chips):
        slot = 2 * i + core
        for k in range(parts):
            side(slot, k).wait_send()
            pl.when((i <= chip) & (chip < chips - 1))(lambda: up(slot, k).wait_send())
            pl.when((i >= chip) & (chip > 0))(lambda: down(slot, k).wait_send())


def convolve(scale, signal, long_filter, padded, taps, shifted, total, wide, midway):
    blocks = signal.shape[1]
    step = min(2 * SHIFTS, blocks)
    padded[0:SHIFTS, :] = jnp.zeros((SHIFTS, LANES), jnp.float32)
    taps[0:8, :] = jnp.zeros((8, LANES), jnp.float32)
    row = lax.broadcasted_iota(jnp.int32, (LANES, LANES), 0)
    lane = lax.broadcasted_iota(jnp.int32, (LANES, LANES), 1)
    causal = lane >= row

    def rolled(block):
        line = jnp.broadcast_to(taps[8 + block : 9 + block, :], (LANES, LANES))
        return pltpu.roll(line, 0, 1, stride=1, stride_axis=0)

    def channel(j, carry):
        midway(j)
        padded[SHIFTS:, :] = signal[j]
        taps[8:, :] = long_filter[j]
        for shift in range(SHIFTS):
            shifted[:, shift * LANES : (shift + 1) * LANES] = padded[
                SHIFTS - shift : SHIFTS - shift + blocks, :
            ].astype(jnp.bfloat16)
        for start in range(0, blocks, step):
            height = blocks - start
            spans = range(start, min(start + step, blocks), SHIFTS)
            last = [rolled(span - 1) for span in spans]
            partial = None
            for shift in range(0, SHIFTS, 2):
                tiles = []
                for extra in range(2):
                    here = [rolled(span + shift + extra) for span in spans]
                    tiles.append(
                        jnp.concatenate(
                            [jnp.where(causal, h, b).astype(jnp.bfloat16) for h, b in zip(here, last)], axis=1
                        )
                    )
                    last = here
                term = jnp.dot(
                    shifted[0:height, shift * LANES : (shift + 2) * LANES],
                    jnp.concatenate(tiles, axis=0),
                    preferred_element_type=jnp.float32,
                )
                partial = term if partial is None else partial + term
            if start == 0:
                total[...] = partial[:, :LANES]
            else:
                total[start:, :] += partial[:, :LANES]
            if len(spans) > 1:
                total[start + SHIFTS :, :] += partial[: height - SHIFTS, LANES:]
        wide[pl.ds(j, blocks, stride=GROUP), :] = total[...] * scale
        return carry

    lax.fori_loop(0, GROUP, channel, 0)


def body(seq_size, tp_size, branches, short_taps, skip_gain, long_filter, out_weight):
    rows, channels = long_filter.shape
    weight_rows, columns = out_weight.shape
    nz, nx, ny = ring_sizes(seq_size)
    assert channels == GROUP * seq_size and nz == tp_size and nx * ny * weight_rows == channels
    halves = rows // LANES
    blocks = halves * seq_size
    columns_a = columns // 4
    slots = (seq_size, halves * GROUP, LANES)
    f32, b16 = jnp.float32, jnp.bfloat16
    dma = pltpu.SemaphoreType.DMA
    steps = nz // 2 + 1
    parts = channels // min(LANES, channels)
    scale = 1.0 / math.sqrt(float(rows * seq_size))
    return pl.pallas_call(
        functools.partial(block_kernel, scale),
        out_shape=jax.ShapeDtypeStruct((rows, columns), b16),
        in_specs=[pl.BlockSpec(memory_space=pltpu.VMEM)] * 5,
        out_specs=pl.BlockSpec(memory_space=pltpu.VMEM),
        scratch_shapes=[
            pltpu.VMEM((3, 16, channels), b16),
            pltpu.VMEM((3, 16 + rows, min(LANES, channels)), f32),
            *[pltpu.VMEM(slots, b16)] * 5,
            pltpu.VMEM((blocks * GROUP, LANES), f32),
            *[pltpu.VMEM((rows, channels), f32)] * 2,
            *[pltpu.VMEM((GROUP, blocks, LANES), f32)] * 2,
            pltpu.VMEM((SHIFTS + blocks, LANES), f32),
            pltpu.VMEM((8 + blocks, LANES), f32),
            pltpu.VMEM((blocks, SHIFTS * LANES), b16),
            pltpu.VMEM((blocks, LANES), f32),
            pltpu.VMEM((nz, nx, ny, weight_rows, columns_a), b16),
            pltpu.VMEM((nx, nz, ny, weight_rows, columns - columns_a), b16),
            pltpu.VMEM((tp_size, rows, channels), b16),
            pltpu.VMEM((rows, columns), f32),
            pltpu.SemaphoreType.REGULAR((2,)),
            dma((2,)),
            dma((6,)),
            dma((4,)),
            dma((nx,)),
            dma((nx,)),
            *[dma((2, steps))] * 4,
            *[dma((2, nz))] * 2,
            *[dma((2,))] * 2,
            dma((parts,)),
            dma((3, tp_size, parts)),
            dma((tp_size, parts)),
        ],
        compiler_params=pltpu.CompilerParams(has_side_effects=True, collective_id=0, vmem_limit_bytes=40 << 20),
        name="hyena",
    )(branches, short_taps, skip_gain[None, :], long_filter, out_weight)


def solution(mesh):
    in_specs = (P(None, "seq", "tp"), P(None, None, "tp"), P("tp"), P("seq", "tp"), P("seq", "tp"))
    return jax.shard_map(
        functools.partial(body, mesh.shape["seq"], mesh.shape["tp"]),
        mesh=mesh,
        in_specs=in_specs,
        out_specs=P("seq", "tp"),
        check_vma=False,
    )
```

```python
import functools
import math

import jax
import jax.numpy as jnp
from jax import lax
from jax.experimental import pallas as pl
from jax.experimental.pallas import tpu as pltpu
from jax.sharding import PartitionSpec as P

MESH = pl.DeviceIdType.MESH
LANES = 128
GROUP = 8
REACH = 32
TURN = 16
PART_A = 2
SCHEDULE = {
    "halo": ("y", "as", "b1"),
    "sent": ("b2",),
    "filter": ("b3",),
    "signal": ("b4", "a1", "n0", "n1", "n2"),
    1: ("b5", "n3", "n4"),
    4: ("a2",),
    "back": ("bl",),
    "gated": ("a3",),
    "passed 1": ("a4",),
    "passed 2": ("a5", "bd"),
}


def ring_sizes(seq_size):
    return (seq_size // 8, 4, 2) if seq_size >= 32 else (seq_size // 4, 2, 2)


def place(seq_size):
    nz, nx, ny = ring_sizes(seq_size)
    me = lax.axis_index("seq")
    return me // (nx * ny), (me // ny) % nx, me % ny


def remote(src, dst, send_sem, recv_sem, device_id):
    return pltpu.make_async_remote_copy(
        src_ref=src,
        dst_ref=dst,
        send_sem=send_sem,
        recv_sem=recv_sem,
        device_id=device_id,
        device_id_type=MESH,
    )


def scatter_start(send, land, send_sem, recv_sem):
    count = send.shape[0]
    me = lax.axis_index("seq")

    def step(t, carry):
        peer = lax.rem(me + t, count)
        remote(send.at[peer], land.at[me], send_sem, recv_sem, {"seq": peer}).start()
        return carry

    lax.fori_loop(1, count, step, 0)
    land[me] = send[me]


def scatter_wait(send, land, send_sem, recv_sem):
    others = pl.ds(0, send.shape[0] - 1)
    copy = remote(send.at[others], land.at[others], send_sem, recv_sem, {"seq": 0})
    copy.wait_recv()
    return copy


def pack_rows(block_of, halves, send, column, width):
    parts = [block_of(h).T.reshape(width // GROUP, GROUP, LANES) for h in range(halves)]
    send[pl.ds(column // GROUP, width // GROUP)] = jnp.concatenate(parts, axis=1).astype(send.dtype)


def block_kernel(
    scale, branches, taps, gain, long_filter, weight, out,
    halo, extended, send_f, send_s, land_f, land_s, land_b, filters, signal, convolved, gate, direct,
    padded, filter_rows, spread, tiles, partial, carried, weight_a, weight_b, gathered, product,
    round_sems, halo_sems, a2a_sems, y_sems, xa_send, xa_recv, za_send, za_recv, zb_send, zb_recv,
    xb_send, xb_recv, far_send, far_recv, back_recv, tp_send, tp_recv,
):
    seq_size, tp_size = land_f.shape[0], gathered.shape[0]
    nz, nx, ny = ring_sizes(seq_size)
    z, x, y = place(seq_size)
    me, mine = lax.axis_index("seq"), lax.axis_index("tp")
    rows, channels = long_filter.shape
    halves = rows // LANES
    width = min(LANES, channels)
    columns_a = weight_a.shape[-1]

    def at(z, x, y):
        return {"seq": (z * nx + x) * ny + y}

    x_peers = [at(z, lax.rem(x + t, nx), y) for t in range(1, nx)]
    z_peers = [at(lax.rem(z + t, nz), x, y) for t in range(1, nz)]
    tp_peers = [{"tp": mine + 1 - 2 * lax.rem(mine, 2)}]
    tp_peers += [{"tp": lax.rem(mine + t, tp_size)} for t in (2, tp_size - 2)]
    other_y = at(z, x, 1 - y)
    following = {"seq": lax.rem(me + 1, seq_size)}
    leading = {"seq": lax.rem(me + seq_size - 1, seq_size)}

    barrier = pltpu.get_barrier_semaphore()
    greeted = [other_y, following, leading] + x_peers + z_peers + tp_peers
    for peer in greeted:
        pl.semaphore_signal(barrier, inc=1, device_id=peer, device_id_type=MESH)
    weight_a[z, x, y] = weight[:, :columns_a]
    weight_b[x, z, y] = weight[:, columns_a:]
    for column in range(0, channels, width):
        pack_rows(
            lambda h: long_filter[h * LANES : (h + 1) * LANES, column : column + width],
            halves, send_f, column, width,
        )
    pl.semaphore_wait(barrier, len(greeted))
    for peer in x_peers:
        pl.semaphore_signal(round_sems.at[0], inc=1, device_id=peer, device_id_type=MESH)
    halo_copy = remote(
        branches.at[:, pl.ds(rows - 16, 16), :], halo, halo_sems.at[0], halo_sems.at[1], following
    )
    halo_copy.start()
    y_a = remote(weight_a.at[z, x, y], weight_a.at[z, x, y], y_sems.at[0], y_sems.at[1], other_y)
    y_b = remote(weight_b.at[x, z, y], weight_b.at[x, z, y], y_sems.at[2], y_sems.at[3], other_y)
    y_a.start()
    y_b.start()
    pl.semaphore_wait(round_sems.at[0], nx - 1)
    pl.semaphore_signal(round_sems.at[1], inc=1, device_id=other_y, device_id_type=MESH)
    pl.semaphore_wait(round_sems.at[1], 1)

    sent = []
    z_pair = at(lax.rem(z + 1, nz), x, y), at(lax.rem(z + nz - 1, nz), x, y)
    x_pair = at(z, lax.rem(x + 1, nx), y), at(z, lax.rem(x + nx - 1, nx), y)

    def z_block(way, t):
        return lax.rem(z + nz - t, nz) if way == 0 else lax.rem(z + t, nz)

    def a_ring(way, t):
        block = z_block(way, t - 1)
        piece = weight_a.at[block, pl.ds(way * (nx // 2), nx // 2)] if 2 * t == nz else weight_a.at[block]
        return remote(piece, piece, za_send.at[way, t], za_recv.at[way, t], z_pair[way])

    def b_ring(way, t):
        block = z_block(way, t - 1)
        piece = weight_b.at[x, block, way] if 2 * t == nz else weight_b.at[x, block]
        return remote(piece, piece, zb_send.at[way, t], zb_recv.at[way, t], z_pair[way])

    def b_next(way, block):
        piece = weight_b.at[x, block]
        return remote(piece, piece, xb_send.at[way, block], xb_recv.at[way, block], x_pair[way])

    def b_far(way):
        source = lax.rem(x + nx - 1, nx) if way == 0 else lax.rem(x + 1, nx)
        piece = weight_b.at[source, pl.ds(way * (nz // 2), nz // 2)]
        return remote(piece, piece, far_send.at[way], far_recv.at[way], x_pair[way])

    def y_done():
        y_a.wait()
        y_b.wait()

    def a_spread():
        for t, peer in enumerate(x_peers):
            copy = remote(weight_a.at[z, x], weight_a.at[z, x], xa_send.at[t], xa_recv.at[x], peer)
            copy.start()
            sent.append(copy)

    def a_step(t):
        if t == 1:
            for i in range(1, nx):
                source = lax.rem(x + nx - i, nx)
                arrived = weight_a.at[z, source]
                remote(arrived, arrived, xa_send.at[0], xa_recv.at[source], other_y).wait_recv()
        for way in range(2):
            if t > 1:
                a_ring(way, t - 1).wait_recv()
        for way in range(2):
            if 2 * t <= nz:
                a_ring(way, t).start()

    def b_step(t):
        for way in range(2):
            if t > 1:
                b_ring(way, t - 1).wait_recv()
        for way in range(2):
            if 2 * t <= nz:
                b_ring(way, t).start()

    def b_along(t):
        for block in [z_block(0, t)] if t == 0 or 2 * t == nz else [z_block(0, t), z_block(1, t)]:
            for way in range(2):
                b_next(way, block).start()

    def b_last():
        for way in range(2):
            for block in range(nz):
                b_next(way, block).wait_recv()
        for way in range(2):
            b_far(way).start()

    def b_done():
        for way in range(2):
            b_far(way).wait_recv()

    steps = {"y": y_done, "as": a_spread, "bl": b_last, "bd": b_done}
    for t in range(1, nz // 2 + 2):
        steps[f"a{t}"] = functools.partial(a_step, t)
        steps[f"b{t}"] = functools.partial(b_step, t)
        steps[f"n{t - 1}"] = functools.partial(b_along, t - 1)

    def weight_steps(point):
        for name in SCHEDULE.get(point, ()):
            steps[name]()

    def pump(j):
        for channel in range(GROUP):
            if channel in SCHEDULE:
                pl.when(j == channel)(functools.partial(weight_steps, channel))

    scatter_start(send_f, land_f, a2a_sems.at[0], a2a_sems.at[1])
    halo_copy.wait()
    weight_steps("halo")
    first = me == 0
    for column in range(0, channels, width):
        span = slice(column, column + width)
        mixed = []
        for branch in range(3):
            before = halo[branch, :, span].astype(jnp.float32)
            extended[branch, 0:16, :] = jnp.where(first, 0.0, before)
            extended[branch, 16:, :] = branches[branch, :, span].astype(jnp.float32)
            mix = taps[0, branch : branch + 1, span] * extended[branch, 16 : 16 + rows, :]
            for lag in (1, 2):
                mix += taps[lag, branch : branch + 1, span] * extended[branch, 16 - lag : 16 - lag + rows, :]
            mixed.append(mix)
        made = mixed[1] * mixed[2]
        gate[:, span] = mixed[0]
        direct[:, span] = gain[0:1, span] * made
        pack_rows(lambda h: made[h * LANES : (h + 1) * LANES], halves, send_s, column, width)
    scatter_start(send_s, land_s, a2a_sems.at[2], a2a_sems.at[3])
    weight_steps("sent")
    copy_f = scatter_wait(send_f, land_f, a2a_sems.at[0], a2a_sems.at[1])
    sent.append(copy_f)
    weight_steps("filter")
    filters[...] = land_f[...].astype(jnp.float32).reshape(filters.shape)
    copy_s = scatter_wait(send_s, land_s, a2a_sems.at[2], a2a_sems.at[3])
    weight_steps("signal")
    signal[...] = land_s[...].astype(jnp.float32).reshape(signal.shape)
    convolve(scale, signal, filters, padded, filter_rows, spread, tiles, partial, carried, convolved, pump)
    copy_s.wait_send()
    send_s[...] = convolved[...].reshape(send_s.shape).astype(send_s.dtype)
    parts = tp_send.shape[2]
    per_part = seq_size // parts
    my_part = me // per_part

    def part_at(k):
        return lax.rem(my_part + parts - k, parts)

    for k in range(parts):

        def send_back(i, carry):
            peer = lax.rem(my_part + k, parts) * per_part + lax.rem(me + i, per_part)
            remote(send_s.at[peer], land_b.at[me], a2a_sems.at[4], back_recv.at[my_part], {"seq": peer}).start()
            return carry

        lax.fori_loop(1 if k == 0 else 0, per_part, send_back, 0)
    land_b[me] = send_s[me]
    sent.append(remote(send_s.at[pl.ds(1, seq_size - 1)], land_b.at[pl.ds(1, seq_size - 1)], a2a_sems.at[4], a2a_sems.at[5], other_y))
    weight_steps("back")

    chips = tp_size // 2
    chip, core = mine // 2, lax.rem(mine, 2)

    def tp_copy(slot, k, kind, to):
        piece = gathered.at[slot, :, pl.ds(pl.multiple_of(part_at(k) * width, width), width)]
        return remote(piece, piece, tp_send.at[kind, slot, k], tp_recv.at[slot, k], {"tp": to})

    def up(slot, k):
        return tp_copy(slot, k, 0, mine + 2)

    def down(slot, k):
        return tp_copy(slot, k, 1, mine - 2)

    def side(slot, k):
        return tp_copy(slot, k, 2, mine + 1 - 2 * core)

    for k in range(parts):
        part = part_at(k)
        landed = land_b.at[pl.ds(part * per_part, per_part - 1 if k == 0 else per_part)]
        remote(landed, landed, a2a_sems.at[4], back_recv.at[part], other_y).wait_recv()
        arrived = land_b[pl.ds(part * per_part, per_part)].astype(jnp.float32)
        columns = pl.ds(pl.multiple_of(part * width, width), width)
        for h in range(halves):
            block = arrived[:, h * GROUP : (h + 1) * GROUP, :].reshape(width, LANES).T
            span = (pl.ds(h * LANES, LANES), columns)
            gathered[mine, h * LANES : (h + 1) * LANES, columns] = (
                gate[span] * (block + direct[span])
            ).astype(gathered.dtype)
        pl.when(chip < chips - 1)(lambda: up(mine, k).start())
        pl.when(chip > 0)(lambda: down(mine, k).start())
        side(mine, k).start()
    weight_steps("gated")

    def pass_on(t):
        for k in range(parts):

            @pl.when(chip >= t)
            def _():
                slot = mine - 2 * t
                side(slot, k).wait_recv()
                pl.when(chip < chips - 1)(lambda: up(slot, k).start())
                side(slot, k).start()

            @pl.when(chip + t < chips)
            def _():
                slot = mine + 2 * t
                side(slot, k).wait_recv()
                pl.when(chip > 0)(lambda: down(slot, k).start())
                side(slot, k).start()

    def add(slot):
        for tile, span in (
            (weight_a[slot], slice(0, columns_a)),
            (weight_b[:, slot], slice(columns_a, columns_a + weight_b.shape[-1])),
        ):
            product[:, span] += jnp.dot(
                gathered[slot], tile.reshape(channels, tile.shape[-1]), preferred_element_type=jnp.float32
            )

    def add_pair(slot):
        other = slot + 1 - 2 * core
        for k in range(parts):
            side(other, k).wait_recv()
        add(slot)
        add(other)

    def add_all(t):
        pl.when(chip >= t)(lambda: add_pair(mine - 2 * t))
        if t > 0:
            pl.when(chip + t < chips)(lambda: add_pair(mine + 2 * t))

    product[...] = jnp.zeros_like(product)
    for t in range(1, chips):
        pass_on(t)
        weight_steps(f"passed {t}")
        if t == chips - 2:
            add_all(0)
    for t in range(1, chips):
        add_all(t)
    out[...] = product[...].astype(out.dtype)

    for copy in sent:
        copy.wait_send()
    for way in range(2):
        for t in range(1, nz // 2 + 1):
            a_ring(way, t).wait_send()
            b_ring(way, t).wait_send()
        for block in range(nz):
            b_next(way, block).wait_send()
        b_far(way).wait_send()
    for i in range(chips):
        slot = 2 * i + core
        for k in range(parts):
            side(slot, k).wait_send()
            pl.when((i <= chip) & (chip < chips - 1))(lambda: up(slot, k).wait_send())
            pl.when((i >= chip) & (chip > 0))(lambda: down(slot, k).wait_send())


def convolve(scale, signal, long_filter, padded, taps, spread, tiles, partial, carried, out, midway):
    blocks = signal.shape[0] // GROUP
    groups = LANES // REACH
    heads = 2 * groups
    padded[0:TURN, :] = jnp.zeros((TURN, LANES), jnp.float32)
    taps[0:8, :] = jnp.zeros((8, LANES), jnp.float32)
    carried[0:8, :] = jnp.zeros((8, LANES), jnp.float32)
    lane = lax.broadcasted_iota(jnp.int32, (blocks, LANES), 1)
    tile_row = lax.broadcasted_iota(jnp.int32, (TURN, LANES), 0)
    tile_lane = lax.broadcasted_iota(jnp.int32, (TURN, LANES), 1)

    def rolled(block):
        line = jnp.broadcast_to(taps[8 + block : 9 + block, :], (TURN, LANES))
        return pltpu.roll(line, 0, 1, stride=1, stride_axis=0)

    def channel(j, carry):
        midway(j)
        padded[TURN:, :] = signal[pl.ds(j, blocks, stride=GROUP), :]
        taps[8:, :] = long_filter[pl.ds(j, blocks, stride=GROUP), :]
        for side in range(2):
            turned = []
            for v in range(groups):
                head = groups * side + v
                moved = padded[TURN - head : TURN - head + blocks, :].astype(jnp.bfloat16)
                turned.append([pltpu.roll(moved, REACH * d, 1) if d else moved for d in range(groups)])
            for i in range(groups):
                tile = turned[0][-i % groups]
                for v in range(1, groups):
                    tile = jnp.where(lane >= REACH * v, turned[v][(v - i) % groups], tile)
                spread[i, :, side * LANES : (side + 1) * LANES] = tile
        last, last_low = rolled(-1), jnp.zeros((TURN, LANES), jnp.bfloat16)
        for block in range(blocks):
            here = rolled(block)
            top = jnp.where(tile_lane >= tile_row, here, last).astype(jnp.bfloat16)
            low = pltpu.roll(top, TURN, 1)
            tail, head = block // heads, block % heads
            tiles[tail // 2, head * REACH : (head + 1) * REACH, (tail % 2) * LANES : (tail % 2 + 1) * LANES] = (
                jnp.concatenate([top, jnp.where(tile_lane >= TURN, low, last_low)], axis=0)
            )
            last, last_low = here, low
        for pair in range(tiles.shape[0]):
            start = 2 * heads * pair
            height = blocks - start
            term = jnp.dot(
                spread[:, 0:height, :].reshape(groups * height, 2 * LANES),
                tiles[pair],
                preferred_element_type=jnp.float32,
            ).reshape(groups, height, 2 * LANES)
            if pair == 0:
                partial[...] = term[:, :, :LANES]
            else:
                partial[:, start:, :] += term[:, :, :LANES]
            partial[:, start + heads :, :] += term[:, : height - heads, LANES:]
        stay, over = partial[0], None
        for i in range(1, groups):
            turned = pltpu.roll(partial[i], REACH * i, 1)
            inside = lane >= REACH * i
            stay += jnp.where(inside, turned, 0.0)
            beyond = jnp.where(inside, 0.0, turned)
            over = beyond if over is None else over + beyond
        carried[8:, :] = over
        out[pl.ds(j, blocks, stride=GROUP), :] = (stay + carried[7 : 7 + blocks, :]) * scale
        return carry

    lax.fori_loop(0, GROUP, channel, 0)


def body(seq_size, tp_size, branches, short_taps, skip_gain, long_filter, out_weight):
    rows, channels = long_filter.shape
    weight_rows, columns = out_weight.shape
    nz, nx, ny = ring_sizes(seq_size)
    assert channels == GROUP * seq_size and nz == tp_size and nx * ny * weight_rows == channels
    halves = rows // LANES
    blocks = halves * seq_size
    columns_a = columns // PART_A
    slots = (seq_size, halves * GROUP, LANES)
    f32, b16 = jnp.float32, jnp.bfloat16
    dma = pltpu.SemaphoreType.DMA
    steps = nz // 2 + 1
    parts = channels // min(LANES, channels)
    scale = 1.0 / math.sqrt(float(rows * seq_size))
    return pl.pallas_call(
        functools.partial(block_kernel, scale),
        out_shape=jax.ShapeDtypeStruct((rows, columns), b16),
        in_specs=[pl.BlockSpec(memory_space=pltpu.VMEM)] * 5,
        out_specs=pl.BlockSpec(memory_space=pltpu.VMEM),
        scratch_shapes=[
            pltpu.VMEM((3, 16, channels), b16),
            pltpu.VMEM((3, 16 + rows, min(LANES, channels)), f32),
            *[pltpu.VMEM(slots, b16)] * 5,
            *[pltpu.VMEM((blocks * GROUP, LANES), f32)] * 3,
            *[pltpu.VMEM((rows, channels), f32)] * 2,
            pltpu.VMEM((TURN + blocks, LANES), f32),
            pltpu.VMEM((8 + blocks, LANES), f32),
            pltpu.VMEM((LANES // REACH, blocks, 2 * LANES), b16),
            pltpu.VMEM((blocks * REACH // (2 * LANES) // 2, 2 * LANES, 2 * LANES), b16),
            pltpu.VMEM((LANES // REACH, blocks, LANES), f32),
            pltpu.VMEM((8 + blocks, LANES), f32),
            pltpu.VMEM((nz, nx, ny, weight_rows, columns_a), b16),
            pltpu.VMEM((nx, nz, ny, weight_rows, columns - columns_a), b16),
            pltpu.VMEM((tp_size, rows, channels), b16),
            pltpu.VMEM((rows, columns), f32),
            pltpu.SemaphoreType.REGULAR((2,)),
            dma((2,)),
            dma((6,)),
            dma((4,)),
            dma((nx,)),
            dma((nx,)),
            *[dma((2, steps))] * 4,
            *[dma((2, nz))] * 2,
            *[dma((2,))] * 2,
            dma((parts,)),
            dma((3, tp_size, parts)),
            dma((tp_size, parts)),
        ],
        compiler_params=pltpu.CompilerParams(has_side_effects=True, collective_id=0, vmem_limit_bytes=40 << 20),
        name="hyena",
    )(branches, short_taps, skip_gain[None, :], long_filter, out_weight)


def solution(mesh):
    in_specs = (P(None, "seq", "tp"), P(None, None, "tp"), P("tp"), P("seq", "tp"), P("seq", "tp"))
    return jax.shard_map(
        functools.partial(body, mesh.shape["seq"], mesh.shape["tp"]),
        mesh=mesh,
        in_specs=in_specs,
        out_specs=P("seq", "tp"),
        check_vma=False,
    )
```

```python
import functools
import math

import jax
import jax.numpy as jnp
from jax import lax
from jax.experimental import pallas as pl
from jax.experimental.pallas import tpu as pltpu
from jax.sharding import PartitionSpec as P

MESH = pl.DeviceIdType.MESH
LANES = 128
GROUP = 8
REACH = 32
TURN = 16
UNROLL = 4
PART_A = 2
SCHEDULE = {
    "halo": ("y", "as", "b1"),
    "sent": ("b2", "n0"),
    "filter": ("b3",),
    "signal": ("b4", "a1", "n1", "n2"),
    3: ("b5", "n3", "n4"),
    6: ("a2",),
    "gated": ("a3", "bl"),
    "passed 1": ("a4",),
    "passed 2": ("a5", "bd"),
}


def ring_sizes(seq_size):
    return (seq_size // 8, 4, 2) if seq_size >= 32 else (seq_size // 4, 2, 2)


def place(seq_size):
    nz, nx, ny = ring_sizes(seq_size)
    me = lax.axis_index("seq")
    return me // (nx * ny), (me // ny) % nx, me % ny


def remote(src, dst, send_sem, recv_sem, device_id):
    return pltpu.make_async_remote_copy(
        src_ref=src,
        dst_ref=dst,
        send_sem=send_sem,
        recv_sem=recv_sem,
        device_id=device_id,
        device_id_type=MESH,
    )


def scatter_start(send, land, send_sem, recv_sem):
    count = send.shape[0]
    me = lax.axis_index("seq")

    def step(t, carry):
        peer = lax.rem(me + t, count)
        remote(send.at[peer], land.at[me], send_sem, recv_sem, {"seq": peer}).start()
        return carry

    lax.fori_loop(1, count, step, 0, unroll=UNROLL)
    land[me] = send[me]


def scatter_wait(send, land, send_sem, recv_sem):
    others = pl.ds(0, send.shape[0] - 1)
    copy = remote(send.at[others], land.at[others], send_sem, recv_sem, {"seq": 0})
    copy.wait_recv()
    return copy


def pack_rows(block_of, halves, send, slot, width):
    parts = [block_of(h).T.reshape(width // GROUP, GROUP, LANES) for h in range(halves)]
    send[pl.ds(slot, width // GROUP)] = jnp.concatenate(parts, axis=1).astype(send.dtype)


def block_kernel(
    scale, branches, taps, gain, long_filter, weight, out,
    halo, extended, send_f, send_s, land_f, land_s, land_b, filters, signal, convolved, gate, direct,
    padded, filter_rows, spread, tiles, partial, carried, weight_a, weight_b, gathered, product,
    round_sems, halo_sems, a2a_sems, y_sems, xa_send, xa_recv, za_send, za_recv, zb_send, zb_recv,
    xb_send, xb_recv, far_send, far_recv, back_recv, tp_send, tp_recv,
):
    seq_size, tp_size = land_f.shape[0], gathered.shape[0]
    nz, nx, ny = ring_sizes(seq_size)
    z, x, y = place(seq_size)
    me, mine = lax.axis_index("seq"), lax.axis_index("tp")
    rows, channels = long_filter.shape
    halves = rows // LANES
    width = min(LANES, channels)
    columns_a = weight_a.shape[-1]

    def at(z, x, y):
        return {"seq": (z * nx + x) * ny + y}

    x_peers = [at(z, lax.rem(x + t, nx), y) for t in range(1, nx)]
    z_peers = [at(lax.rem(z + t, nz), x, y) for t in range(1, nz)]
    tp_peers = [{"tp": mine + 1 - 2 * lax.rem(mine, 2)}]
    tp_peers += [{"tp": lax.rem(mine + t, tp_size)} for t in (2, tp_size - 2)]
    other_y = at(z, x, 1 - y)
    following = {"seq": lax.rem(me + 1, seq_size)}
    leading = {"seq": lax.rem(me + seq_size - 1, seq_size)}

    barrier = pltpu.get_barrier_semaphore()
    greeted = [other_y, following, leading] + x_peers + z_peers + tp_peers
    for peer in greeted:
        pl.semaphore_signal(barrier, inc=1, device_id=peer, device_id_type=MESH)
    weight_a[z, x, y] = weight[:, :columns_a]
    weight_b[x, z, y] = weight[:, columns_a:]
    for column in range(0, channels, width):
        pack_rows(
            lambda h: long_filter[h * LANES : (h + 1) * LANES, column : column + width],
            halves, send_f, column // GROUP, width,
        )
    pl.semaphore_wait(barrier, len(greeted))
    for peer in x_peers:
        pl.semaphore_signal(round_sems.at[0], inc=1, device_id=peer, device_id_type=MESH)
    halo_copy = remote(
        branches.at[:, pl.ds(rows - 16, 16), :], halo, halo_sems.at[0], halo_sems.at[1], following
    )
    halo_copy.start()
    y_a = remote(weight_a.at[z, x, y], weight_a.at[z, x, y], y_sems.at[0], y_sems.at[1], other_y)
    y_b = remote(weight_b.at[x, z, y], weight_b.at[x, z, y], y_sems.at[2], y_sems.at[3], other_y)
    y_a.start()
    y_b.start()
    pl.semaphore_wait(round_sems.at[0], nx - 1)
    pl.semaphore_signal(round_sems.at[1], inc=1, device_id=other_y, device_id_type=MESH)
    pl.semaphore_wait(round_sems.at[1], 1)

    sent = []
    z_pair = at(lax.rem(z + 1, nz), x, y), at(lax.rem(z + nz - 1, nz), x, y)
    x_pair = at(z, lax.rem(x + 1, nx), y), at(z, lax.rem(x + nx - 1, nx), y)

    def z_block(way, t):
        return lax.rem(z + nz - t, nz) if way == 0 else lax.rem(z + t, nz)

    def a_ring(way, t):
        block = z_block(way, t - 1)
        piece = weight_a.at[block, pl.ds(way * (nx // 2), nx // 2)] if 2 * t == nz else weight_a.at[block]
        return remote(piece, piece, za_send.at[way, t], za_recv.at[way, t], z_pair[way])

    def b_ring(way, t):
        block = z_block(way, t - 1)
        piece = weight_b.at[x, block, way] if 2 * t == nz else weight_b.at[x, block]
        return remote(piece, piece, zb_send.at[way, t], zb_recv.at[way, t], z_pair[way])

    def b_next(way, block):
        piece = weight_b.at[x, block]
        return remote(piece, piece, xb_send.at[way, block], xb_recv.at[way, block], x_pair[way])

    def b_far(way):
        source = lax.rem(x + nx - 1, nx) if way == 0 else lax.rem(x + 1, nx)
        piece = weight_b.at[source, pl.ds(way * (nz // 2), nz // 2)]
        return remote(piece, piece, far_send.at[way], far_recv.at[way], x_pair[way])

    def y_done():
        y_a.wait()
        y_b.wait()

    def a_spread():
        for t, peer in enumerate(x_peers):
            copy = remote(weight_a.at[z, x], weight_a.at[z, x], xa_send.at[t], xa_recv.at[x], peer)
            copy.start()
            sent.append(copy)

    def a_step(t):
        if t == 1:
            for i in range(1, nx):
                source = lax.rem(x + nx - i, nx)
                arrived = weight_a.at[z, source]
                remote(arrived, arrived, xa_send.at[0], xa_recv.at[source], other_y).wait_recv()
        for way in range(2):
            if t > 1:
                a_ring(way, t - 1).wait_recv()
        for way in range(2):
            if 2 * t <= nz:
                a_ring(way, t).start()

    def b_step(t):
        for way in range(2):
            if t > 1:
                b_ring(way, t - 1).wait_recv()
        for way in range(2):
            if 2 * t <= nz:
                b_ring(way, t).start()

    def b_along(t):
        for block in [z_block(0, t)] if t == 0 or 2 * t == nz else [z_block(0, t), z_block(1, t)]:
            for way in range(2):
                b_next(way, block).start()

    def b_last():
        for way in range(2):
            for block in range(nz):
                b_next(way, block).wait_recv()
        for way in range(2):
            b_far(way).start()

    def b_done():
        for way in range(2):
            b_far(way).wait_recv()

    steps = {"y": y_done, "as": a_spread, "bl": b_last, "bd": b_done}
    for t in range(1, nz // 2 + 2):
        steps[f"a{t}"] = functools.partial(a_step, t)
        steps[f"b{t}"] = functools.partial(b_step, t)
        steps[f"n{t - 1}"] = functools.partial(b_along, t - 1)

    def weight_steps(point):
        for name in SCHEDULE.get(point, ()):
            steps[name]()

    def pump(j):
        for channel in range(GROUP):
            if channel in SCHEDULE:
                pl.when(j == channel)(functools.partial(weight_steps, channel))

    scatter_start(send_f, land_f, a2a_sems.at[0], a2a_sems.at[1])
    halo_copy.wait()
    weight_steps("halo")
    first = me == 0
    parts = tp_send.shape[2]
    per_part = seq_size // parts
    my_part = me // per_part

    def part_start(k, send, land, send_sem, recv_sem):
        def step(i, carry):
            peer = lax.rem(my_part + k, parts) * per_part + lax.rem(me + i, per_part)
            remote(send.at[peer], land.at[me], send_sem, recv_sem, {"seq": peer}).start()
            return carry

        lax.fori_loop(1 if k == 0 else 0, per_part, step, 0, unroll=UNROLL)

    for k in range(parts):
        part = lax.rem(my_part + k, parts)
        span = pl.ds(pl.multiple_of(part * width, width), width)
        mixed = []
        for branch in range(3):
            before = halo[branch, :, span].astype(jnp.float32)
            extended[branch, 0:16, :] = jnp.where(first, 0.0, before)
            extended[branch, 16:, :] = branches[branch, :, span].astype(jnp.float32)
            mix = taps[0, branch : branch + 1, span] * extended[branch, 16 : 16 + rows, :]
            for lag in (1, 2):
                mix += taps[lag, branch : branch + 1, span] * extended[branch, 16 - lag : 16 - lag + rows, :]
            mixed.append(mix)
        made = mixed[1] * mixed[2]
        gate[:, span] = mixed[0]
        direct[:, span] = gain[0:1, span] * made
        pack_rows(lambda h: made[h * LANES : (h + 1) * LANES], halves, send_s, part * per_part, width)
        part_start(k, send_s, land_s, a2a_sems.at[2], a2a_sems.at[3])
    land_s[me] = send_s[me]
    weight_steps("sent")
    copy_f = scatter_wait(send_f, land_f, a2a_sems.at[0], a2a_sems.at[1])
    sent.append(copy_f)
    weight_steps("filter")
    filters[...] = land_f[...].astype(jnp.float32).reshape(filters.shape)
    copy_s = scatter_wait(send_s, land_s, a2a_sems.at[2], a2a_sems.at[3])
    weight_steps("signal")
    signal[...] = land_s[...].astype(jnp.float32).reshape(signal.shape)
    convolve(scale, signal, filters, padded, filter_rows, spread, tiles, partial, carried, convolved, pump)
    copy_s.wait_send()
    send_s[...] = convolved[...].reshape(send_s.shape).astype(send_s.dtype)
    def part_at(k):
        return lax.rem(my_part + parts - k, parts)

    for k in range(parts):
        part_start(k, send_s, land_b, a2a_sems.at[4], back_recv.at[my_part])
    land_b[me] = send_s[me]
    sent.append(remote(send_s.at[pl.ds(1, seq_size - 1)], land_b.at[pl.ds(1, seq_size - 1)], a2a_sems.at[4], a2a_sems.at[5], other_y))
    weight_steps("back")

    chips = tp_size // 2
    chip, core = mine // 2, lax.rem(mine, 2)

    def tp_copy(slot, k, kind, to):
        piece = gathered.at[slot, :, pl.ds(pl.multiple_of(part_at(k) * width, width), width)]
        return remote(piece, piece, tp_send.at[kind, slot, k], tp_recv.at[slot, k], {"tp": to})

    def up(slot, k):
        return tp_copy(slot, k, 0, mine + 2)

    def down(slot, k):
        return tp_copy(slot, k, 1, mine - 2)

    def side(slot, k):
        return tp_copy(slot, k, 2, mine + 1 - 2 * core)

    for k in range(parts):
        part = part_at(k)
        landed = land_b.at[pl.ds(part * per_part, per_part - 1 if k == 0 else per_part)]
        remote(landed, landed, a2a_sems.at[4], back_recv.at[part], other_y).wait_recv()
        arrived = land_b[pl.ds(part * per_part, per_part)].astype(jnp.float32)
        columns = pl.ds(pl.multiple_of(part * width, width), width)
        for h in range(halves):
            block = arrived[:, h * GROUP : (h + 1) * GROUP, :].reshape(width, LANES).T
            span = (pl.ds(h * LANES, LANES), columns)
            gathered[mine, h * LANES : (h + 1) * LANES, columns] = (
                gate[span] * (block + direct[span])
            ).astype(gathered.dtype)
        pl.when(chip < chips - 1)(lambda: up(mine, k).start())
        pl.when(chip > 0)(lambda: down(mine, k).start())
        side(mine, k).start()
    weight_steps("gated")

    def pass_on(t):
        for k in range(parts):

            @pl.when(chip >= t)
            def _():
                slot = mine - 2 * t
                side(slot, k).wait_recv()
                pl.when(chip < chips - 1)(lambda: up(slot, k).start())
                side(slot, k).start()

            @pl.when(chip + t < chips)
            def _():
                slot = mine + 2 * t
                side(slot, k).wait_recv()
                pl.when(chip > 0)(lambda: down(slot, k).start())
                side(slot, k).start()

    def add(slot):
        for tile, span in (
            (weight_a[slot], slice(0, columns_a)),
            (weight_b[:, slot], slice(columns_a, columns_a + weight_b.shape[-1])),
        ):
            product[:, span] += jnp.dot(
                gathered[slot], tile.reshape(channels, tile.shape[-1]), preferred_element_type=jnp.float32
            )

    def add_pair(slot):
        other = slot + 1 - 2 * core
        for k in range(parts):
            side(other, k).wait_recv()
        add(slot)
        add(other)

    def add_all(t):
        pl.when(chip >= t)(lambda: add_pair(mine - 2 * t))
        if t > 0:
            pl.when(chip + t < chips)(lambda: add_pair(mine + 2 * t))

    product[...] = jnp.zeros_like(product)
    for t in range(1, chips):
        pass_on(t)
        weight_steps(f"passed {t}")
        if t == chips - 2:
            add_all(0)
    for t in range(1, chips):
        add_all(t)
    out[...] = product[...].astype(out.dtype)

    for copy in sent:
        copy.wait_send()
    for way in range(2):
        for t in range(1, nz // 2 + 1):
            a_ring(way, t).wait_send()
            b_ring(way, t).wait_send()
        for block in range(nz):
            b_next(way, block).wait_send()
        b_far(way).wait_send()
    for i in range(chips):
        slot = 2 * i + core
        for k in range(parts):
            side(slot, k).wait_send()
            pl.when((i <= chip) & (chip < chips - 1))(lambda: up(slot, k).wait_send())
            pl.when((i >= chip) & (chip > 0))(lambda: down(slot, k).wait_send())


def convolve(scale, signal, long_filter, padded, taps, spread, tiles, partial, carried, out, midway):
    blocks = signal.shape[0] // GROUP
    groups = LANES // REACH
    heads = 2 * groups
    padded[0:TURN, :] = jnp.zeros((TURN, LANES), jnp.float32)
    taps[0:8, :] = jnp.zeros((8, LANES), jnp.float32)
    carried[0:8, :] = jnp.zeros((8, LANES), jnp.float32)
    lane = lax.broadcasted_iota(jnp.int32, (blocks, LANES), 1)
    tile_row = lax.broadcasted_iota(jnp.int32, (TURN, LANES), 0)
    tile_lane = lax.broadcasted_iota(jnp.int32, (TURN, LANES), 1)

    def rolled(block):
        line = jnp.broadcast_to(taps[8 + block : 9 + block, :], (TURN, LANES))
        return pltpu.roll(line, 0, 1, stride=1, stride_axis=0)

    def channel(j, carry):
        midway(j)
        padded[TURN:, :] = signal[pl.ds(j, blocks, stride=GROUP), :]
        taps[8:, :] = long_filter[pl.ds(j, blocks, stride=GROUP), :]
        for side in range(2):
            turned = []
            for v in range(groups):
                head = groups * side + v
                moved = padded[TURN - head : TURN - head + blocks, :].astype(jnp.bfloat16)
                turned.append([pltpu.roll(moved, REACH * d, 1) if d else moved for d in range(groups)])
            for i in range(groups):
                tile = turned[0][-i % groups]
                for v in range(1, groups):
                    tile = jnp.where(lane >= REACH * v, turned[v][(v - i) % groups], tile)
                spread[i, :, side * LANES : (side + 1) * LANES] = tile
        last, last_low = rolled(-1), jnp.zeros((TURN, LANES), jnp.bfloat16)
        for block in range(blocks):
            here = rolled(block)
            top = jnp.where(tile_lane >= tile_row, here, last).astype(jnp.bfloat16)
            low = pltpu.roll(top, TURN, 1)
            tail, head = block // heads, block % heads
            tiles[tail // 2, head * REACH : (head + 1) * REACH, (tail % 2) * LANES : (tail % 2 + 1) * LANES] = (
                jnp.concatenate([top, jnp.where(tile_lane >= TURN, low, last_low)], axis=0)
            )
            last, last_low = here, low
        for pair in range(tiles.shape[0]):
            start = 2 * heads * pair
            height = blocks - start
            term = jnp.dot(
                spread[:, 0:height, :].reshape(groups * height, 2 * LANES),
                tiles[pair],
                preferred_element_type=jnp.float32,
            ).reshape(groups, height, 2 * LANES)
            if pair == 0:
                partial[...] = term[:, :, :LANES]
            else:
                partial[:, start:, :] += term[:, :, :LANES]
            partial[:, start + heads :, :] += term[:, : height - heads, LANES:]
        stay, over = partial[0], None
        for i in range(1, groups):
            turned = pltpu.roll(partial[i], REACH * i, 1)
            inside = lane >= REACH * i
            stay += jnp.where(inside, turned, 0.0)
            beyond = jnp.where(inside, 0.0, turned)
            over = beyond if over is None else over + beyond
        carried[8:, :] = over
        out[pl.ds(j, blocks, stride=GROUP), :] = (stay + carried[7 : 7 + blocks, :]) * scale
        return carry

    lax.fori_loop(0, GROUP, channel, 0)


def body(seq_size, tp_size, branches, short_taps, skip_gain, long_filter, out_weight):
    rows, channels = long_filter.shape
    weight_rows, columns = out_weight.shape
    nz, nx, ny = ring_sizes(seq_size)
    assert channels == GROUP * seq_size and nz == tp_size and nx * ny * weight_rows == channels
    halves = rows // LANES
    blocks = halves * seq_size
    columns_a = columns // PART_A
    slots = (seq_size, halves * GROUP, LANES)
    f32, b16 = jnp.float32, jnp.bfloat16
    dma = pltpu.SemaphoreType.DMA
    steps = nz // 2 + 1
    parts = channels // min(LANES, channels)
    scale = 1.0 / math.sqrt(float(rows * seq_size))
    return pl.pallas_call(
        functools.partial(block_kernel, scale),
        out_shape=jax.ShapeDtypeStruct((rows, columns), b16),
        in_specs=[pl.BlockSpec(memory_space=pltpu.VMEM)] * 5,
        out_specs=pl.BlockSpec(memory_space=pltpu.VMEM),
        scratch_shapes=[
            pltpu.VMEM((3, 16, channels), b16),
            pltpu.VMEM((3, 16 + rows, min(LANES, channels)), f32),
            *[pltpu.VMEM(slots, b16)] * 5,
            *[pltpu.VMEM((blocks * GROUP, LANES), f32)] * 3,
            *[pltpu.VMEM((rows, channels), f32)] * 2,
            pltpu.VMEM((TURN + blocks, LANES), f32),
            pltpu.VMEM((8 + blocks, LANES), f32),
            pltpu.VMEM((LANES // REACH, blocks, 2 * LANES), b16),
            pltpu.VMEM((blocks * REACH // (2 * LANES) // 2, 2 * LANES, 2 * LANES), b16),
            pltpu.VMEM((LANES // REACH, blocks, LANES), f32),
            pltpu.VMEM((8 + blocks, LANES), f32),
            pltpu.VMEM((nz, nx, ny, weight_rows, columns_a), b16),
            pltpu.VMEM((nx, nz, ny, weight_rows, columns - columns_a), b16),
            pltpu.VMEM((tp_size, rows, channels), b16),
            pltpu.VMEM((rows, columns), f32),
            pltpu.SemaphoreType.REGULAR((2,)),
            dma((2,)),
            dma((6,)),
            dma((4,)),
            dma((nx,)),
            dma((nx,)),
            *[dma((2, steps))] * 4,
            *[dma((2, nz))] * 2,
            *[dma((2,))] * 2,
            dma((parts,)),
            dma((3, tp_size, parts)),
            dma((tp_size, parts)),
        ],
        compiler_params=pltpu.CompilerParams(has_side_effects=True, collective_id=0, vmem_limit_bytes=40 << 20),
        name="hyena",
    )(branches, short_taps, skip_gain[None, :], long_filter, out_weight)


def solution(mesh):
    in_specs = (P(None, "seq", "tp"), P(None, None, "tp"), P("tp"), P("seq", "tp"), P("seq", "tp"))
    return jax.shard_map(
        functools.partial(body, mesh.shape["seq"], mesh.shape["tp"]),
        mesh=mesh,
        in_specs=in_specs,
        out_specs=P("seq", "tp"),
        check_vma=False,
    )
```

```python
import functools
import math

import jax
import jax.numpy as jnp
from jax import lax
from jax.experimental import pallas as pl
from jax.experimental.pallas import tpu as pltpu
from jax.sharding import PartitionSpec as P

MESH = pl.DeviceIdType.MESH
LANES = 128
GROUP = 8
REACH = 32
TURN = 16
UNROLL = 4
PART_A = 2
SCHEDULE = {
    "halo": ("y", "as", "b1"),
    "sent": ("b2", "n0"),
    "filter": ("b3",),
    "signal": ("b4", "a1", "n1", "n2"),
    3: ("b5", "n3", "n4"),
    6: ("a2",),
    "gated": ("a3", "bl"),
    "passed 1": ("a4",),
    "passed 2": ("a5", "bd"),
}


def ring_sizes(seq_size):
    return (seq_size // 8, 4, 2) if seq_size >= 32 else (seq_size // 4, 2, 2)


def place(seq_size):
    nz, nx, ny = ring_sizes(seq_size)
    me = lax.axis_index("seq")
    return me // (nx * ny), (me // ny) % nx, me % ny


def remote(src, dst, send_sem, recv_sem, device_id):
    return pltpu.make_async_remote_copy(
        src_ref=src,
        dst_ref=dst,
        send_sem=send_sem,
        recv_sem=recv_sem,
        device_id=device_id,
        device_id_type=MESH,
    )


def scatter_start(send, land, send_sem, recv_sem):
    count = send.shape[0]
    me = lax.axis_index("seq")

    def step(t, carry):
        peer = lax.rem(me + t, count)
        remote(send.at[peer], land.at[me], send_sem, recv_sem, {"seq": peer}).start()
        return carry

    lax.fori_loop(1, count, step, 0, unroll=UNROLL)
    land[me] = send[me]


def scatter_wait(send, land, send_sem, recv_sem):
    others = pl.ds(0, send.shape[0] - 1)
    copy = remote(send.at[others], land.at[others], send_sem, recv_sem, {"seq": 0})
    copy.wait_recv()
    return copy


def pack_rows(block_of, halves, send, slot, width):
    parts = [block_of(h).T.reshape(width // GROUP, GROUP, LANES) for h in range(halves)]
    send[pl.ds(slot, width // GROUP)] = jnp.concatenate(parts, axis=1).astype(send.dtype)


def block_kernel(
    scale, branches, taps, gain, long_filter, weight, out,
    halo, extended, send_f, send_s, land_f, land_s, land_b, filters, signal, convolved, gate, direct,
    padded, filter_rows, spread, tiles, partial, carried, weight_a, weight_b, gathered, product,
    round_sems, halo_sems, a2a_sems, y_sems, xa_send, xa_recv, za_send, za_recv, zb_send, zb_recv,
    xb_send, xb_recv, far_send, far_recv, back_recv, tp_send, tp_recv,
):
    seq_size, tp_size = land_f.shape[0], gathered.shape[0]
    nz, nx, ny = ring_sizes(seq_size)
    z, x, y = place(seq_size)
    me, mine = lax.axis_index("seq"), lax.axis_index("tp")
    rows, channels = long_filter.shape
    halves = rows // LANES
    width = min(LANES, channels)
    columns_a = weight_a.shape[-1]

    def at(z, x, y):
        return {"seq": (z * nx + x) * ny + y}

    x_peers = [at(z, lax.rem(x + t, nx), y) for t in range(1, nx)]
    z_peers = [at(lax.rem(z + t, nz), x, y) for t in range(1, nz)]
    tp_peers = [{"tp": mine + 1 - 2 * lax.rem(mine, 2)}]
    tp_peers += [{"tp": lax.rem(mine + t, tp_size)} for t in (2, tp_size - 2)]
    other_y = at(z, x, 1 - y)
    following = {"seq": lax.rem(me + 1, seq_size)}
    leading = {"seq": lax.rem(me + seq_size - 1, seq_size)}

    barrier = pltpu.get_barrier_semaphore()
    greeted = [other_y, following, leading] + x_peers + z_peers + tp_peers
    for peer in greeted:
        pl.semaphore_signal(barrier, inc=1, device_id=peer, device_id_type=MESH)
    weight_a[z, x, y] = weight[:, :columns_a]
    weight_b[x, z, y] = weight[:, columns_a:]
    for column in range(0, channels, width):
        pack_rows(
            lambda h: long_filter[h * LANES : (h + 1) * LANES, column : column + width],
            halves, send_f, column // GROUP, width,
        )
    pl.semaphore_wait(barrier, len(greeted))
    for peer in x_peers:
        pl.semaphore_signal(round_sems.at[0], inc=1, device_id=peer, device_id_type=MESH)
    halo_copy = remote(
        branches.at[:, pl.ds(rows - 16, 16), :], halo, halo_sems.at[0], halo_sems.at[1], following
    )
    halo_copy.start()
    y_a = remote(weight_a.at[z, x, y], weight_a.at[z, x, y], y_sems.at[0], y_sems.at[1], other_y)
    y_b = remote(weight_b.at[x, z, y], weight_b.at[x, z, y], y_sems.at[2], y_sems.at[3], other_y)
    y_a.start()
    y_b.start()
    pl.semaphore_wait(round_sems.at[0], nx - 1)
    pl.semaphore_signal(round_sems.at[1], inc=1, device_id=other_y, device_id_type=MESH)
    pl.semaphore_wait(round_sems.at[1], 1)

    sent = []
    z_pair = at(lax.rem(z + 1, nz), x, y), at(lax.rem(z + nz - 1, nz), x, y)
    x_pair = at(z, lax.rem(x + 1, nx), y), at(z, lax.rem(x + nx - 1, nx), y)

    def z_block(way, t):
        return lax.rem(z + nz - t, nz) if way == 0 else lax.rem(z + t, nz)

    def a_ring(way, t):
        block = z_block(way, t - 1)
        piece = weight_a.at[block, pl.ds(way * (nx // 2), nx // 2)] if 2 * t == nz else weight_a.at[block]
        return remote(piece, piece, za_send.at[way, t], za_recv.at[way, t], z_pair[way])

    def b_ring(way, t):
        block = z_block(way, t - 1)
        piece = weight_b.at[x, block, way] if 2 * t == nz else weight_b.at[x, block]
        return remote(piece, piece, zb_send.at[way, t], zb_recv.at[way, t], z_pair[way])

    def b_next(way, block):
        piece = weight_b.at[x, block]
        return remote(piece, piece, xb_send.at[way, block], xb_recv.at[way, block], x_pair[way])

    def b_far(way):
        source = lax.rem(x + nx - 1, nx) if way == 0 else lax.rem(x + 1, nx)
        piece = weight_b.at[source, pl.ds(way * (nz // 2), nz // 2)]
        return remote(piece, piece, far_send.at[way], far_recv.at[way], x_pair[way])

    def y_done():
        y_a.wait()
        y_b.wait()

    def a_spread():
        for t, peer in enumerate(x_peers):
            copy = remote(weight_a.at[z, x], weight_a.at[z, x], xa_send.at[t], xa_recv.at[x], peer)
            copy.start()
            sent.append(copy)

    def a_step(t):
        if t == 1:
            for i in range(1, nx):
                source = lax.rem(x + nx - i, nx)
                arrived = weight_a.at[z, source]
                remote(arrived, arrived, xa_send.at[0], xa_recv.at[source], other_y).wait_recv()
        for way in range(2):
            if t > 1:
                a_ring(way, t - 1).wait_recv()
        for way in range(2):
            if 2 * t <= nz:
                a_ring(way, t).start()

    def b_step(t):
        for way in range(2):
            if t > 1:
                b_ring(way, t - 1).wait_recv()
        for way in range(2):
            if 2 * t <= nz:
                b_ring(way, t).start()

    def b_along(t):
        for block in [z_block(0, t)] if t == 0 or 2 * t == nz else [z_block(0, t), z_block(1, t)]:
            for way in range(2):
                b_next(way, block).start()

    def b_last():
        for way in range(2):
            for block in range(nz):
                b_next(way, block).wait_recv()
        for way in range(2):
            b_far(way).start()

    def b_done():
        for way in range(2):
            b_far(way).wait_recv()

    steps = {"y": y_done, "as": a_spread, "bl": b_last, "bd": b_done}
    for t in range(1, nz // 2 + 2):
        steps[f"a{t}"] = functools.partial(a_step, t)
        steps[f"b{t}"] = functools.partial(b_step, t)
        steps[f"n{t - 1}"] = functools.partial(b_along, t - 1)

    def weight_steps(point):
        for name in SCHEDULE.get(point, ()):
            steps[name]()

    def pump(j):
        for channel in range(GROUP):
            if channel in SCHEDULE:
                pl.when(j == channel)(functools.partial(weight_steps, channel))

    scatter_start(send_f, land_f, a2a_sems.at[0], a2a_sems.at[1])
    halo_copy.wait()
    weight_steps("halo")
    first = me == 0
    parts = tp_send.shape[2]
    per_part = seq_size // parts
    my_part = me // per_part

    def part_start(k, send, land, send_sem, recv_sem):
        def step(i, carry):
            peer = lax.rem(my_part + k, parts) * per_part + lax.rem(me + i, per_part)
            remote(send.at[peer], land.at[me], send_sem, recv_sem, {"seq": peer}).start()
            return carry

        lax.fori_loop(1 if k == 0 else 0, per_part, step, 0, unroll=UNROLL)

    for k in range(parts):
        part = lax.rem(my_part + k, parts)
        span = pl.ds(pl.multiple_of(part * width, width), width)
        mixed = []
        for branch in range(3):
            before = halo[branch, :, span].astype(jnp.float32)
            extended[branch, 0:16, :] = jnp.where(first, 0.0, before)
            extended[branch, 16:, :] = branches[branch, :, span].astype(jnp.float32)
            mix = taps[0, branch : branch + 1, span] * extended[branch, 16 : 16 + rows, :]
            for lag in (1, 2):
                mix += taps[lag, branch : branch + 1, span] * extended[branch, 16 - lag : 16 - lag + rows, :]
            mixed.append(mix)
        made = mixed[1] * mixed[2]
        gate[:, span] = mixed[0]
        direct[:, span] = gain[0:1, span] * made
        pack_rows(lambda h: made[h * LANES : (h + 1) * LANES], halves, send_s, part * per_part, width)
        part_start(k, send_s, land_s, a2a_sems.at[2], a2a_sems.at[3])
    land_s[me] = send_s[me]
    weight_steps("sent")
    copy_f = scatter_wait(send_f, land_f, a2a_sems.at[0], a2a_sems.at[1])
    sent.append(copy_f)
    weight_steps("filter")
    filters[...] = land_f[...].astype(jnp.float32).reshape(filters.shape)
    copy_s = scatter_wait(send_s, land_s, a2a_sems.at[2], a2a_sems.at[3])
    weight_steps("signal")
    signal[...] = land_s[...].astype(jnp.float32).reshape(signal.shape)
    convolve(scale, signal, filters, padded, filter_rows, spread, tiles, partial, carried, convolved, pump)
    copy_s.wait_send()
    send_s[...] = convolved[...].reshape(send_s.shape).astype(send_s.dtype)
    def part_at(k):
        return lax.rem(my_part + parts - k, parts)

    for k in range(parts):
        part_start(k, send_s, land_b, a2a_sems.at[4], back_recv.at[my_part])
    land_b[me] = send_s[me]
    sent.append(remote(send_s.at[pl.ds(1, seq_size - 1)], land_b.at[pl.ds(1, seq_size - 1)], a2a_sems.at[4], a2a_sems.at[5], other_y))
    weight_steps("back")

    chips = tp_size // 2
    chip, core = mine // 2, lax.rem(mine, 2)

    def tp_copy(slot, k, kind, to):
        piece = gathered.at[slot, :, pl.ds(pl.multiple_of(part_at(k) * width, width), width)]
        return remote(piece, piece, tp_send.at[kind, slot, k], tp_recv.at[slot, k], {"tp": to})

    def up(slot, k):
        return tp_copy(slot, k, 0, mine + 2)

    def down(slot, k):
        return tp_copy(slot, k, 1, mine - 2)

    def side(slot, k):
        return tp_copy(slot, k, 2, mine + 1 - 2 * core)

    for k in range(parts):
        part = part_at(k)
        landed = land_b.at[pl.ds(part * per_part, per_part - 1 if k == 0 else per_part)]
        remote(landed, landed, a2a_sems.at[4], back_recv.at[part], other_y).wait_recv()
        arrived = land_b[pl.ds(part * per_part, per_part)].astype(jnp.float32)
        columns = pl.ds(pl.multiple_of(part * width, width), width)
        for h in range(halves):
            block = arrived[:, h * GROUP : (h + 1) * GROUP, :].reshape(width, LANES).T
            span = (pl.ds(h * LANES, LANES), columns)
            gathered[mine, h * LANES : (h + 1) * LANES, columns] = (
                gate[span] * (block + direct[span])
            ).astype(gathered.dtype)
        pl.when(chip < chips - 1)(lambda: up(mine, k).start())
        pl.when(chip > 0)(lambda: down(mine, k).start())
        side(mine, k).start()
    weight_steps("gated")

    def pass_on(t):
        for k in range(parts):

            @pl.when(chip >= t)
            def _():
                slot = mine - 2 * t
                side(slot, k).wait_recv()
                pl.when(chip < chips - 1)(lambda: up(slot, k).start())
                side(slot, k).start()

            @pl.when(chip + t < chips)
            def _():
                slot = mine + 2 * t
                side(slot, k).wait_recv()
                pl.when(chip > 0)(lambda: down(slot, k).start())
                side(slot, k).start()

    def add(slot):
        for tile, span in (
            (weight_a[slot], slice(0, columns_a)),
            (weight_b[:, slot], slice(columns_a, columns_a + weight_b.shape[-1])),
        ):
            product[:, span] += jnp.dot(
                gathered[slot], tile.reshape(channels, tile.shape[-1]), preferred_element_type=jnp.float32
            )

    def add_pair(slot):
        other = slot + 1 - 2 * core
        for k in range(parts):
            side(other, k).wait_recv()
        add(slot)
        add(other)

    def add_all(t):
        pl.when(chip >= t)(lambda: add_pair(mine - 2 * t))
        if t > 0:
            pl.when(chip + t < chips)(lambda: add_pair(mine + 2 * t))

    product[...] = jnp.zeros_like(product)
    for t in range(1, chips):
        pass_on(t)
        weight_steps(f"passed {t}")
        if t == chips - 2:
            add_all(0)
            add_all(1)
    for t in range(2, chips):
        add_all(t)
    out[...] = product[...].astype(out.dtype)

    for copy in sent:
        copy.wait_send()
    for way in range(2):
        for t in range(1, nz // 2 + 1):
            a_ring(way, t).wait_send()
            b_ring(way, t).wait_send()
        for block in range(nz):
            b_next(way, block).wait_send()
        b_far(way).wait_send()
    for i in range(chips):
        slot = 2 * i + core
        for k in range(parts):
            side(slot, k).wait_send()
            pl.when((i <= chip) & (chip < chips - 1))(lambda: up(slot, k).wait_send())
            pl.when((i >= chip) & (chip > 0))(lambda: down(slot, k).wait_send())


def convolve(scale, signal, long_filter, padded, taps, spread, tiles, partial, carried, out, midway):
    blocks = signal.shape[0] // GROUP
    groups = LANES // REACH
    heads = 2 * groups
    padded[0:TURN, :] = jnp.zeros((TURN, LANES), jnp.float32)
    taps[0:8, :] = jnp.zeros((8, LANES), jnp.float32)
    carried[0:8, :] = jnp.zeros((8, LANES), jnp.float32)
    lane = lax.broadcasted_iota(jnp.int32, (blocks, LANES), 1)
    tile_row = lax.broadcasted_iota(jnp.int32, (TURN, LANES), 0)
    tile_lane = lax.broadcasted_iota(jnp.int32, (TURN, LANES), 1)

    def rolled(block):
        line = jnp.broadcast_to(taps[8 + block : 9 + block, :], (TURN, LANES))
        return pltpu.roll(line, 0, 1, stride=1, stride_axis=0)

    def channel(j, carry):
        midway(j)
        padded[TURN:, :] = signal[pl.ds(j, blocks, stride=GROUP), :]
        taps[8:, :] = long_filter[pl.ds(j, blocks, stride=GROUP), :]
        for side in range(2):
            turned = []
            for v in range(groups):
                head = groups * side + v
                moved = padded[TURN - head : TURN - head + blocks, :].astype(jnp.bfloat16)
                turned.append([pltpu.roll(moved, REACH * d, 1) if d else moved for d in range(groups)])
            for i in range(groups):
                tile = turned[0][-i % groups]
                for v in range(1, groups):
                    tile = jnp.where(lane >= REACH * v, turned[v][(v - i) % groups], tile)
                spread[i, :, side * LANES : (side + 1) * LANES] = tile
        last, last_low = rolled(-1), jnp.zeros((TURN, LANES), jnp.bfloat16)
        for block in range(blocks):
            here = rolled(block)
            top = jnp.where(tile_lane >= tile_row, here, last).astype(jnp.bfloat16)
            low = pltpu.roll(top, TURN, 1)
            tail, head = block // heads, block % heads
            tiles[tail // 2, head * REACH : (head + 1) * REACH, (tail % 2) * LANES : (tail % 2 + 1) * LANES] = (
                jnp.concatenate([top, jnp.where(tile_lane >= TURN, low, last_low)], axis=0)
            )
            last, last_low = here, low
        for pair in range(tiles.shape[0]):
            start = 2 * heads * pair
            height = blocks - start
            term = jnp.dot(
                spread[:, 0:height, :].reshape(groups * height, 2 * LANES),
                tiles[pair],
                preferred_element_type=jnp.float32,
            ).reshape(groups, height, 2 * LANES)
            if pair == 0:
                partial[...] = term[:, :, :LANES]
            else:
                partial[:, start:, :] += term[:, :, :LANES]
            partial[:, start + heads :, :] += term[:, : height - heads, LANES:]
        stay, over = partial[0], None
        for i in range(1, groups):
            turned = pltpu.roll(partial[i], REACH * i, 1)
            inside = lane >= REACH * i
            stay += jnp.where(inside, turned, 0.0)
            beyond = jnp.where(inside, 0.0, turned)
            over = beyond if over is None else over + beyond
        carried[8:, :] = over
        out[pl.ds(j, blocks, stride=GROUP), :] = (stay + carried[7 : 7 + blocks, :]) * scale
        return carry

    lax.fori_loop(0, GROUP, channel, 0)


def body(seq_size, tp_size, branches, short_taps, skip_gain, long_filter, out_weight):
    rows, channels = long_filter.shape
    weight_rows, columns = out_weight.shape
    nz, nx, ny = ring_sizes(seq_size)
    assert channels == GROUP * seq_size and nz == tp_size and nx * ny * weight_rows == channels
    halves = rows // LANES
    blocks = halves * seq_size
    columns_a = columns // PART_A
    slots = (seq_size, halves * GROUP, LANES)
    f32, b16 = jnp.float32, jnp.bfloat16
    dma = pltpu.SemaphoreType.DMA
    steps = nz // 2 + 1
    parts = channels // min(LANES, channels)
    scale = 1.0 / math.sqrt(float(rows * seq_size))
    return pl.pallas_call(
        functools.partial(block_kernel, scale),
        out_shape=jax.ShapeDtypeStruct((rows, columns), b16),
        in_specs=[pl.BlockSpec(memory_space=pltpu.VMEM)] * 5,
        out_specs=pl.BlockSpec(memory_space=pltpu.VMEM),
        scratch_shapes=[
            pltpu.VMEM((3, 16, channels), b16),
            pltpu.VMEM((3, 16 + rows, min(LANES, channels)), f32),
            *[pltpu.VMEM(slots, b16)] * 5,
            *[pltpu.VMEM((blocks * GROUP, LANES), f32)] * 3,
            *[pltpu.VMEM((rows, channels), f32)] * 2,
            pltpu.VMEM((TURN + blocks, LANES), f32),
            pltpu.VMEM((8 + blocks, LANES), f32),
            pltpu.VMEM((LANES // REACH, blocks, 2 * LANES), b16),
            pltpu.VMEM((blocks * REACH // (2 * LANES) // 2, 2 * LANES, 2 * LANES), b16),
            pltpu.VMEM((LANES // REACH, blocks, LANES), f32),
            pltpu.VMEM((8 + blocks, LANES), f32),
            pltpu.VMEM((nz, nx, ny, weight_rows, columns_a), b16),
            pltpu.VMEM((nx, nz, ny, weight_rows, columns - columns_a), b16),
            pltpu.VMEM((tp_size, rows, channels), b16),
            pltpu.VMEM((rows, columns), f32),
            pltpu.SemaphoreType.REGULAR((2,)),
            dma((2,)),
            dma((6,)),
            dma((4,)),
            dma((nx,)),
            dma((nx,)),
            *[dma((2, steps))] * 4,
            *[dma((2, nz))] * 2,
            *[dma((2,))] * 2,
            dma((parts,)),
            dma((3, tp_size, parts)),
            dma((tp_size, parts)),
        ],
        compiler_params=pltpu.CompilerParams(has_side_effects=True, collective_id=0, vmem_limit_bytes=40 << 20),
        name="hyena",
    )(branches, short_taps, skip_gain[None, :], long_filter, out_weight)


def solution(mesh):
    in_specs = (P(None, "seq", "tp"), P(None, None, "tp"), P("tp"), P("seq", "tp"), P("seq", "tp"))
    return jax.shard_map(
        functools.partial(body, mesh.shape["seq"], mesh.shape["tp"]),
        mesh=mesh,
        in_specs=in_specs,
        out_specs=P("seq", "tp"),
        check_vma=False,
    )
```
